32 devices in a mesh: grp: 2 (over x), seq: 16 (over z, y, core).
Axes of the slice: x: 2, y: 2, z: 4, core: 2. Of those that a mesh axis runs over, the one named last changes fastest.
Arguments:
- hidden: bfloat16 [4, 5120, 1280], P('grp', 'seq'), parts along dimension 0, may hold values from -160 to 160
- mod_shift: float32 [5120], replicated, may hold values from -3 to 3
- mod_scale: float32 [5120], replicated, may hold values from -0.5 to 0.5
- head_weight: float32 [64, 5120], replicated, may hold values from -0.078125 to 0.078125
- head_bias: float32 [64], replicated, may hold values from -3 to 3
- conv_in_weight: bfloat16 [3, 3, 3, 16, 384], replicated, may hold values from -0.3125 to 0.3125
- conv_in_bias: float32 [384], replicated, may hold values from -3 to 3
- gain_in: float32 [384], replicated, may hold values from 0.1 to 1.9
- up_weight: bfloat16 [3, 3, 384, 192], replicated, may hold values from -0.109375 to 0.109375
- up_bias: float32 [192], replicated, may hold values from -3 to 3
- gain_up: float32 [192], replicated, may hold values from 0.1 to 1.9
- out_weight: bfloat16 [3, 3, 3, 192, 96], replicated, may hold values from -0.078125 to 0.078125
- out_bias: float32 [96], replicated, may hold values from -2 to 2
Outputs:
- decoded: bfloat16 [4, 64, 320, 96], P('grp', 'seq'), parts along dimension 0
The draws below stay inside these ranges and needn't reach their ends.
There are 2 independent parts, one for each index of `grp`. The reference program is written for one: setup_inputs(seed, part) draws one part's arguments, and reference() takes and returns one part's arrays. A program takes and returns all parts, laid end to end along the dimension named above; an argument that names none is the same for every part. Nothing has to cross between parts.
All inputs are finite; a program needn't handle non-finite values.
Results may differ from the reference program's by a relative error of at most 0.0056.
Values may be sent and summed in bfloat16 or wider, within the bound.
No kernel may reach another device: no remote copies, remote signals or barrier semaphores. Data moves between devices by JAX's collectives and lax.ppermute only.
A program may use at most 64 MiB of HBM per device.

```python
import math
import jax
import jax.numpy as jnp
from jax import lax

D = 5120
LAT = 16
C1 = 384
C2 = 192
C3 = 96
FRAMES = 2
TOK_W = 80
PATCH = 64
TOK_ROWS = 16


def draw_hidden(key, part):
    key_base = jax.random.fold_in(key, 11)
    key_rows = jax.random.fold_in(key, 12)
    key_cols = jax.random.fold_in(key, 13)
    shape_all = (FRAMES, D, TOK_ROWS * TOK_W)
    row_scale = jnp.exp(jax.random.uniform(key_rows, (FRAMES, 1, TOK_ROWS * TOK_W), minval=0.0, maxval=math.log(10.0)))
    col_jitter = jnp.exp(jax.random.uniform(key_cols, (1, D, 1), minval=0.0, maxval=math.log(2.0)))
    position = (jnp.arange(D, dtype=jnp.float32) / D).reshape(1, D, 1)
    base_vals = jnp.clip(jax.random.normal(key_base, shape_all), -4.0, 4.0)
    col_scale = 10.0 ** position * col_jitter * 0.5
    result = base_vals * row_scale * col_scale * 0.3
    return jnp.clip(result, -160.0, 160.0).astype(jnp.bfloat16)


def bell_draw(own_key, extent, deviation, reach, kind=jnp.bfloat16):
    drawn = jax.random.normal(own_key, extent, jnp.float32) * deviation
    return jnp.minimum(jnp.maximum(drawn, -reach), reach).astype(kind)


def setup_inputs(seed: int = 0, part: int = 0) -> dict:
    key_list = jax.random.split(jax.random.key(seed), 14)
    own_keys = jax.random.split(jax.random.fold_in(key_list[13], part), 14)
    return {
        "hidden": draw_hidden(jax.random.fold_in(jax.random.fold_in(key_list[13], part), 71), part),
        "mod_shift": bell_draw(key_list[1], (D,), 0.5, 3.0, jnp.float32),
        "mod_scale": jnp.clip(jax.random.uniform(key_list[2], (D,), jnp.float32, -0.5, 0.5), -0.5, 0.5),
        "head_weight": bell_draw(key_list[3], (PATCH, D), D ** -0.5, 0.078125, jnp.float32),
        "head_bias": bell_draw(key_list[4], (PATCH,), 0.5, 3.0, jnp.float32),
        "conv_in_weight": bell_draw(key_list[5], (3, 3, 3, LAT, C1), (27 * LAT) ** -0.5, 0.3125),
        "conv_in_bias": bell_draw(key_list[6], (C1,), 0.5, 3.0, jnp.float32),
        "gain_in": jnp.clip(1.0 + 0.18 * jax.random.normal(key_list[7], (C1,), jnp.float32), 0.1, 1.9),
        "up_weight": bell_draw(key_list[8], (3, 3, C1, C2), (9 * C1) ** -0.5, 0.109375),
        "up_bias": bell_draw(key_list[9], (C2,), 0.5, 3.0, jnp.float32),
        "gain_up": jnp.clip(1.0 + 0.18 * jax.random.normal(key_list[10], (C2,), jnp.float32), 0.1, 1.9),
        "out_weight": bell_draw(key_list[11], (3, 3, 3, C2, C3), (27 * C2) ** -0.5, 0.078125),
        "out_bias": bell_draw(key_list[12], (C3,), 0.3, 2.0, jnp.float32),
    }


def rms_silu(values, gain_vec):
    squares = lax.optimization_barrier(jnp.mean(values * values, axis=-1, keepdims=True))
    normed = values * lax.rsqrt(squares + 1e-06) * gain_vec
    return normed * jax.nn.sigmoid(normed)

def conv_time(values, weight):
    padded = jnp.pad(values, ((2, 0), (1, 1), (1, 1), (0, 0))).astype(jnp.float32)
    result = lax.conv_general_dilated(padded[None], weight.astype(jnp.float32), (1, 1, 1), 'VALID', dimension_numbers=('NDHWC', 'DHWIO', 'NDHWC'), precision=lax.Precision.HIGHEST)
    return result[0]

def conv_plane(values, weight):
    padded = jnp.pad(values, ((0, 0), (1, 1), (1, 1), (0, 0))).astype(jnp.float32)
    return lax.conv_general_dilated(padded, weight.astype(jnp.float32), (1, 1), 'VALID', dimension_numbers=('NHWC', 'HWIO', 'NHWC'), precision=lax.Precision.HIGHEST)

def unpatch(projected):
    frames, tok_rows, tok_cols, patch_len = projected.shape
    lat_ch = patch_len // 4
    grid = projected.reshape(frames, tok_rows, tok_cols, 2, 2, lat_ch)
    return grid.transpose(0, 1, 3, 2, 4, 5).reshape(frames, 2 * tok_rows, 2 * tok_cols, lat_ch)

def reference(hidden, mod_shift, mod_scale, head_weight, head_bias, conv_in_weight, conv_in_bias, gain_in, up_weight, up_bias, gain_up, out_weight, out_bias):
    values = hidden.astype(jnp.float32)
    token_mean = lax.optimization_barrier(jnp.mean(values, axis=1, keepdims=True))
    centred = values - token_mean
    variance = lax.optimization_barrier(jnp.mean(centred * centred, axis=1, keepdims=True))
    modded = centred * lax.rsqrt(variance + 1e-06) * (1.0 + mod_scale)[:, None] + mod_shift[:, None]
    projected = jnp.einsum('fdt,kd->ftk', modded, head_weight, precision=lax.Precision.HIGHEST) + head_bias
    projected = projected.reshape(FRAMES, TOK_ROWS, TOK_W, PATCH)
    latent = unpatch(projected.astype(jnp.bfloat16))
    first_act = rms_silu(conv_time(latent, conv_in_weight) + conv_in_bias, gain_in).astype(jnp.bfloat16)
    upsampled = jnp.repeat(jnp.repeat(first_act, 2, axis=1), 2, axis=2)
    second_act = rms_silu(conv_plane(upsampled, up_weight) + up_bias, gain_up).astype(jnp.bfloat16)
    return (conv_time(second_act, out_weight) + out_bias).astype(jnp.bfloat16)
```

```python
import functools
import jax
import jax.numpy as jnp
import numpy as np
from jax import lax
from jax.experimental import pallas as pl
from jax.experimental.pallas import tpu as pltpu
from jax.sharding import PartitionSpec as P

TOK_W = 80
HALF = TOK_W // 2
STAT = 4
EPS = 1e-06
HIGH = lax.Precision.HIGHEST
BF = jnp.bfloat16
F32 = jnp.float32


def split(values):
    high = values.astype(BF).astype(F32)
    return high, values - high


def lanes(rows):
    return lax.broadcasted_iota(jnp.int32, (rows, 128), 1)


def project_kernel(hid_ref, w_ref, scale_ref, out_ref):
    feats = hid_ref.shape[1]
    width = hid_ref.shape[2]
    gain = w_ref[...] * (1.0 + scale_ref[...])
    gain = jnp.concatenate([gain[0:16], gain[32:48], gain[16:32], gain[48:64]], axis=0)
    high, low = split(gain)
    gain_sum = jnp.sum(gain, axis=1, keepdims=True)
    stack = jnp.concatenate([high, low, jnp.ones((16, feats), F32)], axis=0).astype(BF)
    parts, stats = [], []
    for f in range(2):
        x = hid_ref[f]
        prod = jnp.dot(stack, x, preferred_element_type=F32)
        mean = prod[128:129] * (1.0 / feats)
        parts.append(prod[0:64] + prod[64:128] - gain_sum * mean)
        off = x.astype(F32) - mean
        second = jnp.sum(off * off, axis=0, keepdims=True)
        m_hi, m_lo = split(mean)
        s_hi, s_lo = split(second)
        stats.append(
            jnp.concatenate([m_hi, m_lo, s_hi, s_lo, jnp.zeros((4, width), F32)], axis=0)
        )
    flat = jnp.concatenate(parts, axis=0).T
    lane = lanes(8)
    for row in range(width // TOK_W):
        for h in range(2):
            at = row * TOK_W + h * HALF
            base = (at // 128) * 128
            wide = min(256, width - base)
            picks = []
            for f in range(2):
                window = stats[f][:, base : base + wide]
                shift = (64 * f - (at - base)) % wide
                if shift:
                    window = pltpu.roll(window, shift, 1)
                picks.append(window[:, :128])
            tail = jnp.where(
                lane < HALF, picks[0], jnp.where((lane >= 64) & (lane < 64 + HALF), picks[1], 0.0)
            )
            out_ref[h, row] = jnp.concatenate([flat[at : at + HALF], tail], axis=0).astype(BF)


def project(hidden, w_slice, scale_slice):
    frames, feats, tokens = hidden.shape
    block = 640
    rows = tokens // TOK_W
    rows_block = block // TOK_W
    return pl.pallas_call(
        project_kernel,
        grid=(tokens // block,),
        in_specs=[
            pl.BlockSpec((frames, feats, block), lambda i: (0, 0, i)),
            pl.BlockSpec((64, feats), lambda i: (0, 0)),
            pl.BlockSpec((1, feats), lambda i: (0, 0)),
        ],
        out_specs=pl.BlockSpec((2, rows_block, 48, 128), lambda i: (0, i, 0, 0)),
        out_shape=jax.ShapeDtypeStruct((2, rows, 48, 128), BF),
        compiler_params=pltpu.CompilerParams(vmem_limit_bytes=32 << 20),
        name="project",
    )(hidden, w_slice, scale_slice)


def prepare_kernel(
    w_ref, scale_ref, shift_ref, hb_ref, dev_ref, cin_ref, up_ref, upv_ref, cout_ref,
    table_ref, const_ref, cin_out, up_out, upv_out, cout_out,
):
    feats = w_ref.shape[1] * 2 // dev_ref.shape[0]
    head = w_ref[...]
    head = jnp.concatenate([head[0:16], head[32:48], head[16:32], head[48:64]], axis=0)
    gain = head * (1.0 + scale_ref[...])
    count = dev_ref.shape[0]
    place = lax.broadcasted_iota(jnp.int32, (count, w_ref.shape[1]), 1) - dev_ref[...] * feats
    inside = ((place >= 0) & (place < feats)).astype(F32)
    dims = (((1,), (1,)), ((), ()))
    sums = lax.dot_general(inside, gain, dims, precision=HIGH, preferred_element_type=F32)
    table_ref[...] = jnp.concatenate([sums, sums], axis=1)
    const = lax.dot_general(
        shift_ref[...], head, dims, precision=HIGH, preferred_element_type=F32
    )
    hb = hb_ref[...]
    hb = jnp.concatenate([hb[:, 0:16], hb[:, 32:48], hb[:, 16:32], hb[:, 48:64]], axis=1)
    const = const + hb
    const_ref[...] = jnp.concatenate([const, const], axis=1)

    zero16 = jnp.zeros((16, 384), BF)
    for tap in range(2):
        for ly in range(4):
            for lx in range(4):
                row = (ly // 2) * 128 + lx * 32 + (ly % 2) * 16
                for qy in range(2):
                    for qx in range(2):
                        dy, dx = ly - qy, lx - qx
                        good = 0 <= dy < 3 and 0 <= dx < 3
                        piece = cin_ref[tap + 1, dy, dx] if good else zero16
                        col = (qy * 2 + qx) * 384
                        cin_out[tap, row : row + 16, col : col + 384] = piece

    taps = {(0, 0): (0, 1), (0, 1): (2,), (1, 0): (0,), (1, 1): (1, 2)}
    lane = lanes(384)
    for dx in range(2):
        for dy in range(2):
            for py in range(2):
                blocks = []
                for px in range(2):
                    total = None
                    for b in taps[py, dy]:
                        for e in taps[px, dx]:
                            term = up_ref[b, e].astype(F32)
                            total = term if total is None else total + term
                    blocks.append(total)
                left, right = blocks
                ends = jnp.concatenate([left[:, 128:192], right[:, 128:192]], axis=1)
                row = (dy * 2 + dx) * 384
                col = py * 384
                up_out[row : row + 384, col : col + 128] = left[:, 0:128].astype(BF)
                up_out[row : row + 384, col + 128 : col + 256] = right[:, 0:128].astype(BF)
                up_out[row : row + 384, col + 256 : col + 384] = ends.astype(BF)
    vec = upv_ref[...]
    piece = jnp.concatenate(
        [vec[:, 0:128], vec[:, 0:128], vec[:, 128:192], vec[:, 128:192]], axis=1
    )
    upv_out[...] = piece

    cout_out[...] = jnp.zeros(cout_out.shape, BF)
    for tap in range(2):
        for b in range(3):
            for v in range(2):
                for s in range(2):
                    for o in range(2):
                        e = 2 * v + s - o
                        if not 0 <= e < 3:
                            continue
                        row = b * 768 + v * 384
                        weight = cout_ref[tap + 1, b, e]
                        lo = row + s * 128
                        hi = row + 256 + s * 64
                        cout_out[tap, lo : lo + 128, o * 128 : o * 128 + 96] = weight[0:128]
                        cout_out[tap, hi : hi + 64, o * 128 : o * 128 + 96] = weight[128:192]


def prepare(head_weight, mod_scale, mod_shift, head_bias, devs, cin, up, upv, cout):
    count = devs.shape[0]
    return pl.pallas_call(
        prepare_kernel,
        out_shape=[
            jax.ShapeDtypeStruct((count, 128), F32),
            jax.ShapeDtypeStruct((1, 128), F32),
            jax.ShapeDtypeStruct((2, 256, 1536), BF),
            jax.ShapeDtypeStruct((1536, 768), BF),
            jax.ShapeDtypeStruct((2, 384), F32),
            jax.ShapeDtypeStruct((2, 2304, 256), BF),
        ],
        compiler_params=pltpu.CompilerParams(vmem_limit_bytes=40 << 20),
        cost_estimate=pl.CostEstimate(
            flops=20_000_000, bytes_accessed=10_000_000, transcendentals=0
        ),
        name="prepare",
    )(head_weight, mod_scale, mod_shift, head_bias, devs, cin, up, upv, cout)


def silu_half(half):
    return half + half * jnp.tanh(half)


def decode_kernel(
    flags_ref, sums_ref, table_ref, const_ref, cin_ref, cinv_ref, up_ref, upv_ref, cout_ref,
    coutv_ref, out_ref, fa, fb, fx, ua, ub, xe, xo, lines,
):
    count = table_ref.shape[0] // 2
    feats = count * 0 + flags_ref.shape[0] * 0
    del feats
    has_low = flags_ref[0]
    has_high = flags_ref[1]
    group = flags_ref[2].astype(F32)
    n_stat = sums_ref.shape[2] - HALF

    pick_row = lax.broadcasted_iota(jnp.int32, (count + 8, n_stat), 0)
    pick_col = lax.broadcasted_iota(jnp.int32, (count + 8, n_stat), 1)
    of_dev, of_kind = pick_col // STAT, pick_col % STAT
    pick = ((of_kind < 2) & (pick_row == of_dev)) | ((of_kind >= 2) & (pick_row == count))
    pick = pick.astype(F32).astype(BF)
    lane40, sub40 = lanes(HALF), lax.broadcasted_iota(jnp.int32, (HALF, 128), 0)
    lane80, sub80 = lanes(TOK_W), lax.broadcasted_iota(jnp.int32, (TOK_W, 128), 0)
    spread_mask = (lane40 % 64) == sub40
    ones_block = (
        (lax.broadcasted_iota(jnp.int32, (128, 128), 0) // 64) == (lanes(128) // 64)
    ).astype(F32)
    edge = [[None] * 3 for _ in range(2)]
    for j in range(3):
        halves = []
        for h in range(2):
            block = sums_ref[h, j]
            stats = jnp.dot(pick, block[HALF:], preferred_element_type=F32)
            means = stats[0:count]
            mean = jnp.sum(means, axis=0, keepdims=True) * (1.0 / count)
            off = means - mean
            total = count * group
            var = (
                stats[count : count + 1] + group * jnp.sum(off * off, axis=0, keepdims=True)
            ) / total
            inv = lax.rsqrt(var + EPS)
            shift = lax.dot_general(
                off, table_ref[h * count : (h + 1) * count], (((0,), (0,)), ((), ())),
                precision=HIGH, preferred_element_type=F32,
            )
            shift = jnp.where(lane40 < 64, shift[0:HALF], shift[64 : 64 + HALF])
            inv_all = jnp.dot(
                jnp.where(spread_mask, inv, 0.0), ones_block,
                precision=HIGH, preferred_element_type=F32,
            )
            halves.append((block[0:HALF].astype(F32) + shift) * inv_all + const_ref[...])
        row = jnp.concatenate(halves, axis=0)
        if j == 0:
            row = jnp.where(has_low > 0, row, 0.0)
        if j == 2:
            row = jnp.where(has_high > 0, row, 0.0)
        swapped = pltpu.roll(row, 64, 1)
        for f in range(2):
            first = lane80 < 64 if f == 0 else lane80 >= 64
            both = pltpu.roll(jnp.where(first, row, swapped), 32, 1)
            before = jnp.where(sub80 == 0, 0.0, pltpu.roll(both, 1, 0))
            after = jnp.where(sub80 == TOK_W - 1, 0.0, pltpu.roll(both, TOK_W - 1, 0))
            edge[f][j] = jnp.where(
                lane80 < 32, before, jnp.where(lane80 >= 96, after, both)
            ).astype(BF)

    def patch(f):
        return jnp.concatenate(
            [jnp.concatenate([edge[f][b], edge[f][b + 1]], axis=1) for b in range(2)], axis=0
        )

    patches = [patch(0), patch(1)]
    bias_in, gain_in = cinv_ref[0:1], cinv_ref[1:2] * 0.5
    sub_one = lax.broadcasted_iota(jnp.int32, (TOK_W, 384), 0)
    zeros_ext = jnp.zeros((TOK_W, 384), F32)
    for f in range(2):
        pre = jnp.dot(patches[f], cin_ref[1], preferred_element_type=F32)
        if f == 1:
            pre = pre + jnp.dot(patches[0], cin_ref[0], preferred_element_type=F32)
        for b in range(2):
            for qy in range(2):
                y = 2 * b + qy
                act = []
                for qx in range(2):
                    col = (qy * 2 + qx) * 384
                    v = pre[b * TOK_W : (b + 1) * TOK_W, col : col + 384] + bias_in
                    mean_sq = jnp.sum(v * v, axis=1, keepdims=True) * (1.0 / 384)
                    a = silu_half(v * lax.rsqrt(mean_sq + EPS) * gain_in)
                    if y == 0:
                        a = jnp.where(has_low > 0, a, 0.0)
                    if y == 3:
                        a = jnp.where(has_high > 0, a, 0.0)
                    act.append(a)
                even, odd = act
                back = jnp.where(sub_one == 0, 0.0, pltpu.roll(odd, 1, 0))
                even, odd, back = even.astype(BF), odd.astype(BF), back.astype(BF)
                for pair, part in ((y - 1, 1), (y, 0)):
                    if not 0 <= pair < 3:
                        continue
                    at = slice((f * 3 + pair) * TOK_W, (f * 3 + pair + 1) * TOK_W)
                    fa[at, part * 768 : part * 768 + 384] = even
                    fa[at, part * 768 + 384 : part * 768 + 768] = odd
                    fb[at, part * 768 : part * 768 + 384] = back
                    fb[at, part * 768 + 384 : part * 768 + 768] = even
                    fx[f * 3 + pair : f * 3 + pair + 1, part * 768 : part * 768 + 384] = act[1][
                        TOK_W - 1 : TOK_W
                    ]
                    fx[f * 3 + pair : f * 3 + pair + 1, part * 768 + 384 : part * 768 + 768] = (
                        zeros_ext[0:1]
                    )
    del sub_one

    ua[...] = jnp.dot(fa[...], up_ref[...], preferred_element_type=F32)
    ub[0 : 6 * TOK_W] = jnp.dot(fb[...], up_ref[...], preferred_element_type=F32)
    extra_in = jnp.where(
        lax.broadcasted_iota(jnp.int32, (8, 1536), 0) < 6, fx[...], 0.0
    )
    extra_in = jnp.concatenate([extra_in, jnp.zeros((8, 1536), F32)], axis=0).astype(BF)
    extra = jnp.dot(extra_in, up_ref[...], preferred_element_type=F32)[0:8]
    bias_up, gain_up = upv_ref[0:1], upv_ref[1:2] * 0.5

    def second(u):
        v = u + bias_up
        t0, t1, t2 = v[:, 0:128], v[:, 128:256], v[:, 256:384]
        lane = lanes(u.shape[0])
        q = t2 * t2
        left = jnp.sum(t0 * t0 + jnp.where(lane < 64, q, 0.0), axis=1, keepdims=True)
        right = jnp.sum(t1 * t1 + jnp.where(lane < 64, 0.0, q), axis=1, keepdims=True)
        left = lax.rsqrt(left * (1.0 / 192) + EPS)
        right = lax.rsqrt(right * (1.0 / 192) + EPS)
        g = gain_up
        return (
            silu_half(t0 * left * g[:, 0:128]),
            silu_half(t1 * right * g[:, 128:256]),
            silu_half(t2 * jnp.where(lane < 64, left, right) * g[:, 256:384]),
        )

    for f in range(2):
        for pair in range(3):
            at = (f * 3 + pair) * TOK_W
            for py in range(2):
                y = pair * 2 + py
                cols = slice(py * 384, py * 384 + 384)

                def keep(value, y=y):
                    if y == 0:
                        return jnp.where(has_low > 0, value, 0.0)
                    if y == 5:
                        return jnp.where(has_high > 0, value, 0.0)
                    return value

                mid = [keep(t) for t in second(ua[at : at + TOK_W, cols])]
                low = [keep(t) for t in second(ub[at : at + TOK_W, cols])]
                end = [keep(t) for t in second(extra[:, cols])]
                to = slice(y * TOK_W, (y + 1) * TOK_W)
                first = sub80 == 0
                low[0] = jnp.where(first, 0.0, low[0])
                low[2] = jnp.where(first & (lane80 < 64), 0.0, low[2])
                end[1] = jnp.zeros_like(end[1])
                end[2] = jnp.where(lanes(8) < 64, end[2], 0.0)
                for k in range(3):
                    m = mid[k].astype(BF)
                    xe[f, to, k * 128 : k * 128 + 128] = low[k].astype(BF)
                    xe[f, to, 384 + k * 128 : 512 + k * 128] = m
                    xo[f, to, k * 128 : k * 128 + 128] = m
                    last = end[k][f * 3 + pair : f * 3 + pair + 1]
                    ahead = jnp.where(
                        sub80 == TOK_W - 1, last, pltpu.roll(low[k], TOK_W - 1, 0)
                    )
                    xo[f, to, 384 + k * 128 : 512 + k * 128] = ahead.astype(BF)

    bias_out = coutv_ref[...]
    for f in range(2):
        for side, x in enumerate((xe, xo)):
            acc = None
            for b in range(3):
                rows = slice(b * TOK_W, (b + 4) * TOK_W)
                ks = slice(b * 768, b * 768 + 768)
                term = jnp.dot(x[f, rows], cout_ref[1, ks], preferred_element_type=F32)
                acc = term if acc is None else acc + term
                if f == 1:
                    acc = acc + jnp.dot(x[0, rows], cout_ref[0, ks], preferred_element_type=F32)
            for j in range(4):
                for o in range(2):
                    lines[j, pl.ds(2 * side + o, TOK_W, stride=4), :] = (
                        acc[j * TOK_W : (j + 1) * TOK_W, o * 128 : o * 128 + 128] + bias_out
                    )
        for j in range(4):
            out_ref[f, j] = lines[j][:, 0:96].astype(BF)


def decode(flags, sums, table, const, cin, cinv, up, upv, cout, coutv):
    vmem = pl.BlockSpec(memory_space=pltpu.VMEM)
    return pl.pallas_call(
        decode_kernel,
        in_specs=[pl.BlockSpec(memory_space=pltpu.SMEM)] + [vmem] * 9,
        out_specs=vmem,
        out_shape=jax.ShapeDtypeStruct((2, 4, 4 * TOK_W, 96), BF),
        scratch_shapes=[
            pltpu.VMEM((6 * TOK_W, 1536), BF),
            pltpu.VMEM((6 * TOK_W, 1536), BF),
            pltpu.VMEM((8, 1536), F32),
            pltpu.VMEM((6 * TOK_W, 768), F32),
            pltpu.VMEM((6 * TOK_W, 768), F32),
            pltpu.VMEM((2, 6 * TOK_W, 768), BF),
            pltpu.VMEM((2, 6 * TOK_W, 768), BF),
            pltpu.VMEM((4, 4 * TOK_W, 128), F32),
        ],
        compiler_params=pltpu.CompilerParams(vmem_limit_bytes=48 << 20),
        cost_estimate=pl.CostEstimate(
            flops=5_000_000_000, bytes_accessed=8_000_000, transcendentals=1_300_000
        ),
        name="decode",
    )(flags, sums, table, const, cin, cinv, up, upv, cout, coutv)


def exchange(block, mask, count):
    return lax.ppermute(block, "seq", [(i, i ^ mask) for i in range(count)])


def merged(own, received):
    total = own[:, :HALF].astype(F32)
    for item in received:
        total = total + item[:, :HALF].astype(F32)
    return jnp.concatenate(
        [total.astype(BF), own[:, HALF:]] + [item[:, HALF:] for item in received], axis=1
    )


def cut(block, start, size):
    return lax.dynamic_slice_in_dim(block, start, size, 0)


def gather_rows(parts, me, count):
    parts = parts[:, :, : HALF + STAT]
    core = me & 1
    own = lax.dynamic_index_in_dim(parts, core, 0, False)
    give = lax.dynamic_index_in_dim(parts, 1 - core, 0, False)
    block = merged(own, [exchange(give, 1, count)])
    order = [0, 1]

    def window(base, size):
        return jnp.clip(base - 1, 0, count - size)

    start = jnp.int32(0)
    bits = count.bit_length() - 1
    bit = bits - 2
    steps = [[2 << bit, 1 << bit, 3 << bit]]
    while bit > 1:
        bit -= 1
        steps.append([1 << bit])
    for masks in steps:
        unit = min(masks)
        size = unit + 2
        base = (me // unit) * unit
        new = window(base, size)
        received = [
            exchange(cut(block, window(base ^ mask, size) - start, size), mask, count)
            for mask in masks
        ]
        block = merged(cut(block, new - start, size), received)
        order = order + [o ^ mask for mask in masks for o in order]
        start = new
    padded = jnp.pad(block, ((1, 1), (0, 0), (0, 0)))
    mine = cut(padded, me - start, 3)
    other = exchange(cut(padded, (me ^ 1) - start, 3), 1, count)
    low = jnp.where(core == 0, mine, other)
    high = jnp.where(core == 0, other, mine)
    return jnp.stack([low, high]), order


def local(
    hidden,
    mod_shift,
    mod_scale,
    head_weight,
    head_bias,
    conv_in_weight,
    conv_in_bias,
    gain_in,
    up_weight,
    up_bias,
    gain_up,
    out_weight,
    out_bias,
):
    count = lax.axis_size("seq")
    me = lax.axis_index("seq")
    feats = hidden.shape[1]
    w_slice = lax.dynamic_slice_in_dim(head_weight, me * feats, feats, 1)
    scale_slice = lax.dynamic_slice_in_dim(mod_scale, me * feats, feats, 0)[None]
    parts = project(hidden, w_slice, scale_slice)
    sums, order = gather_rows(parts, me, count)
    masks = np.asarray(order, np.int32)
    devs = jnp.concatenate([((me // 2) * 2) ^ masks, ((me // 2) * 2 + 1) ^ masks])[:, None]
    table, const, cin, up, upv, cout = prepare(
        head_weight, mod_scale[None], mod_shift[None], head_bias[None], devs,
        conv_in_weight, up_weight, jnp.stack([up_bias, gain_up]), out_weight,
    )
    flags = jnp.stack([(me > 0).astype(jnp.int32), (me < count - 1).astype(jnp.int32), jnp.int32(feats)])
    cinv = jnp.stack([conv_in_bias, gain_in])
    coutv = jnp.pad(out_bias, (0, 32))[None]
    return decode(flags, sums, table, const, cin, cinv, up, upv, cout, coutv)


def solution(mesh):
    placed = (P("grp", "seq", None), P(), P(), P(), P(), P(), P(), P(), P(), P(), P(), P(), P())
    return jax.shard_map(
        local, mesh=mesh, in_specs=placed, out_specs=P("grp", "seq", None, None), check_vma=False
    )
```

```python
import functools
import jax
import jax.numpy as jnp
import numpy as np
from jax import lax
from jax.experimental import pallas as pl
from jax.experimental.pallas import tpu as pltpu
from jax.sharding import PartitionSpec as P

TOK_W = 80
HALF = TOK_W // 2
STAT = 4
EPS = 1e-06
HIGH = lax.Precision.HIGHEST
BF = jnp.bfloat16
F32 = jnp.float32


def in_hbm(value):
    return pltpu.with_memory_space_constraint(value, pltpu.HBM)


def split(values):
    high = values.astype(BF).astype(F32)
    return high, values - high


def lanes(rows):
    return lax.broadcasted_iota(jnp.int32, (rows, 128), 1)


def project_kernel(flags_ref, hid_ref, w_ref, scale_ref, own_ref, give_ref, hid, w, scale, sems):
    frames, feats, tokens = hid_ref.shape
    width = hid.shape[3]
    me = flags_ref[0]
    core = me & 1
    wide = w.shape[1]
    at = jnp.minimum(lax.div(me * feats, 128) * 128, w_ref.shape[1] - wide)
    at = pl.multiple_of(at, 128)
    copies = [
        pltpu.make_async_copy(w_ref.at[:, pl.ds(at, wide)], w, sems.at[0]),
        pltpu.make_async_copy(scale_ref.at[:, pl.ds(at, wide)], scale, sems.at[1]),
    ]
    blocks = tokens // width
    for i in range(blocks):
        copies.append(
            pltpu.make_async_copy(
                hid_ref.at[:, :, pl.ds(i * width, width)], hid.at[i], sems.at[2 + i]
            )
        )
    for copy in copies:
        copy.start()
    copies[0].wait()
    copies[1].wait()
    gain = w[...] * (1.0 + scale[...])
    gain = pltpu.roll(gain, wide - (me * feats - at), 1)[:, :feats]
    gain = jnp.concatenate([gain[0:16], gain[32:48], gain[16:32], gain[48:64]], axis=0)
    high, low = split(gain)
    gain_sum = jnp.sum(gain, axis=1, keepdims=True)
    stack = jnp.concatenate([high, low, jnp.ones((16, feats), F32)], axis=0).astype(BF)
    lane = lanes(8)
    sub = lax.broadcasted_iota(jnp.int32, (8, 128), 0)
    for i in range(blocks):
        copies[2 + i].wait()
        parts, stats = [], []
        for f in range(frames):
            x = hid[i, f]
            prod = jnp.dot(stack, x, preferred_element_type=F32)
            mean = prod[128:129] * (1.0 / feats)
            parts.append(prod[0:64] + prod[64:128] - gain_sum * mean)
            off = x.astype(F32) - mean
            second = jnp.sum(off * off, axis=0, keepdims=True)
            m_hi, m_lo = split(mean)
            s_hi, s_lo = split(second)
            four = jnp.concatenate([m_hi, m_lo, s_hi, s_lo] * 2, axis=0)
            stats.append(four)
        flat = jnp.concatenate(parts, axis=0).T
        for row in range(width // TOK_W):
            pair = []
            for h in range(2):
                first = row * TOK_W + h * HALF
                base = (first // 128) * 128
                span = min(256, width - base)
                picks = []
                for f in range(2):
                    window = stats[f][:, base : base + span]
                    shift = (64 * f - (first - base)) % span
                    if shift:
                        window = pltpu.roll(window, shift, 1)
                    picks.append(window[:, :128])
                tail = jnp.where(
                    lane < HALF,
                    picks[0],
                    jnp.where((lane >= 64) & (lane < 64 + HALF), picks[1], 0.0),
                )
                tail = jnp.where(lax.div(sub, STAT) == core, tail, 0.0)
                pair.append(jnp.concatenate([flat[first : first + HALF], tail], axis=0))
            to = i * (width // TOK_W) + row
            own_ref[to] = jnp.where(core == 0, pair[0], pair[1]).astype(BF)
            give_ref[to] = jnp.where(core == 0, pair[1], pair[0]).astype(BF)


def project(flags, hidden, head_weight, scale):
    frames, feats, tokens = hidden.shape
    width = 640
    rows = tokens // TOK_W
    wide = min(head_weight.shape[1], (feats + 127) // 128 * 128 + 128)
    hbm = pl.BlockSpec(memory_space=pltpu.HBM)
    vmem = pl.BlockSpec(memory_space=pltpu.VMEM)
    return pl.pallas_call(
        project_kernel,
        in_specs=[pl.BlockSpec(memory_space=pltpu.SMEM), hbm, hbm, hbm],
        out_specs=[vmem, vmem],
        out_shape=[jax.ShapeDtypeStruct((rows, HALF + 2 * STAT, 128), BF)] * 2,
        scratch_shapes=[
            pltpu.VMEM((tokens // width, frames, feats, width), BF),
            pltpu.VMEM((64, wide), F32),
            pltpu.VMEM((1, wide), F32),
            pltpu.SemaphoreType.DMA((2 + tokens // width,)),
        ],
        compiler_params=pltpu.CompilerParams(vmem_limit_bytes=16 << 20),
        name="project",
    )(flags, in_hbm(hidden), in_hbm(head_weight), in_hbm(scale))


def prepare_first(cin_ref, cin_out):
    zero16 = jnp.zeros((16, 384), BF)
    for tap in range(2):
        for ly in range(4):
            for lx in range(4):
                row = (ly // 2) * 128 + lx * 32 + (ly % 2) * 16
                for qy in range(2):
                    for qx in range(2):
                        dy, dx = ly - qy, lx - qx
                        good = 0 <= dy < 3 and 0 <= dx < 3
                        piece = cin_ref[tap + 1, dy, dx] if good else zero16
                        col = (qy * 2 + qx) * 384
                        cin_out[tap, row : row + 16, col : col + 384] = piece


def prepare_up(up_ref, up_out):
    taps = {(0, 0): (0, 1), (0, 1): (2,), (1, 0): (0,), (1, 1): (1, 2)}
    for dx in range(2):
        for dy in range(2):
            for py in range(2):
                for px in range(2):
                    total = None
                    for b in taps[py, dy]:
                        for e in taps[px, dx]:
                            term = up_ref[b, e].astype(F32)
                            total = term if total is None else total + term
                    total = total.astype(BF)
                    k = slice((dy * 2 + dx) * 384, (dy * 2 + dx + 1) * 384)
                    n = py * 384
                    up_out[n + px * 128 : n + px * 128 + 128, k] = total[0:128]
                    up_out[n + 256 + px * 64 : n + 320 + px * 64, k] = total[128:192]


def prepare_last(cout_ref, cout_out):
    cout_out[...] = jnp.zeros(cout_out.shape, BF)
    for tap in range(2):
        for b in range(3):
            for v in range(2):
                for s in range(2):
                    for o in range(2):
                        e = 2 * v + s - o
                        if not 0 <= e < 3:
                            continue
                        row = b * 768 + v * 384
                        weight = cout_ref[tap + 1, b, e]
                        lo = row + s * 128
                        hi = row + 256 + s * 64
                        cout_out[tap, lo : lo + 128, o * 128 : o * 128 + 96] = weight[0:128]
                        cout_out[tap, hi : hi + 64, o * 128 : o * 128 + 96] = weight[128:192]


def prepare_kernel(
    w_ref, scale_ref, shift_ref, hb_ref, dev_ref, cin_ref, up_ref, upv_ref, cout_ref,
    table_ref, const_ref, cin_out, up_out, upv_out, cout_out, w, cin, up, cout, sems,
):
    copies = [
        pltpu.make_async_copy(source, target, sems.at[i])
        for i, (source, target) in enumerate(
            ((cin_ref, cin), (up_ref, up), (cout_ref, cout), (w_ref, w))
        )
    ]
    for copy in copies:
        copy.start()
    copies[0].wait()
    prepare_first(cin, cin_out)
    copies[1].wait()
    prepare_up(up, up_out)
    vec = upv_ref[...]
    upv_out[...] = jnp.concatenate(
        [vec[:, 0:128], vec[:, 0:128], vec[:, 128:192], vec[:, 128:192]], axis=1
    )
    copies[2].wait()
    prepare_last(cout, cout_out)
    copies[3].wait()
    feats = w_ref.shape[1] // dev_ref.shape[0]
    head = w[...]
    head = jnp.concatenate([head[0:16], head[32:48], head[16:32], head[48:64]], axis=0)
    gain = head * (1.0 + scale_ref[...])
    count = dev_ref.shape[0]
    place = lax.broadcasted_iota(jnp.int32, (count, w_ref.shape[1]), 1) - dev_ref[...] * feats
    inside = ((place >= 0) & (place < feats)).astype(F32)
    dims = (((1,), (1,)), ((), ()))
    sums = lax.dot_general(inside, gain, dims, precision=HIGH, preferred_element_type=F32)
    table_ref[...] = jnp.concatenate([sums, sums], axis=1)
    const = lax.dot_general(
        shift_ref[...], head, dims, precision=HIGH, preferred_element_type=F32
    )
    hb = hb_ref[...]
    hb = jnp.concatenate([hb[:, 0:16], hb[:, 32:48], hb[:, 16:32], hb[:, 48:64]], axis=1)
    const = const + hb
    const_ref[...] = jnp.concatenate([const, const], axis=1)


def prepare(head_weight, mod_scale, mod_shift, head_bias, devs, cin, up, upv, cout):
    count = devs.shape[0]
    hbm = pl.BlockSpec(memory_space=pltpu.HBM)
    vmem = pl.BlockSpec(memory_space=pltpu.VMEM)
    return pl.pallas_call(
        prepare_kernel,
        in_specs=[hbm, vmem, vmem, vmem, vmem, hbm, hbm, vmem, hbm],
        scratch_shapes=[
            pltpu.VMEM(head_weight.shape, F32),
            pltpu.VMEM(cin.shape, BF),
            pltpu.VMEM(up.shape, BF),
            pltpu.VMEM(cout.shape, BF),
            pltpu.SemaphoreType.DMA((4,)),
        ],
        out_shape=[
            jax.ShapeDtypeStruct((count, 128), F32),
            jax.ShapeDtypeStruct((1, 128), F32),
            jax.ShapeDtypeStruct((2, 256, 1536), BF),
            jax.ShapeDtypeStruct((768, 1536), BF),
            jax.ShapeDtypeStruct((2, 384), F32),
            jax.ShapeDtypeStruct((2, 2304, 256), BF),
        ],
        compiler_params=pltpu.CompilerParams(vmem_limit_bytes=20 << 20),
        cost_estimate=pl.CostEstimate(
            flops=20_000_000, bytes_accessed=10_000_000, transcendentals=0
        ),
        name="prepare",
    )(
        in_hbm(head_weight), mod_scale, mod_shift, head_bias, devs, in_hbm(cin), in_hbm(up), upv,
        in_hbm(cout),
    )


def silu_half(half):
    return half + half * jnp.tanh(half)


def decode_kernel(
    group, flags_ref, sums_ref, table_ref, const_ref, cin_ref, cinv_ref, up_ref, upv_ref, cout_ref,
    coutv_ref, out_ref, fa, fb, fx, ua, ub, xe, xo, lines,
):
    count = table_ref.shape[0]
    has_low = flags_ref[1]
    has_high = flags_ref[2]
    n_stat = sums_ref.shape[2] - HALF

    pick_row = lax.broadcasted_iota(jnp.int32, (count + 8, n_stat), 0)
    pick_col = lax.broadcasted_iota(jnp.int32, (count + 8, n_stat), 1)
    of_dev, of_kind = pick_col // STAT, pick_col % STAT
    pick = ((of_kind < 2) & (pick_row == of_dev)) | ((of_kind >= 2) & (pick_row == count))
    pick = pick.astype(F32).astype(BF)
    lane40, sub40 = lanes(HALF), lax.broadcasted_iota(jnp.int32, (HALF, 128), 0)
    lane80, sub80 = lanes(TOK_W), lax.broadcasted_iota(jnp.int32, (TOK_W, 128), 0)
    spread_mask = (lane40 % 64) == sub40
    ones_block = (
        (lax.broadcasted_iota(jnp.int32, (128, 128), 0) // 64) == (lanes(128) // 64)
    ).astype(F32)
    edge = [[None] * 3 for _ in range(2)]
    for j in range(3):
        halves = []
        for h in range(2):
            block = sums_ref[h, j]
            stats = jnp.dot(pick, block[HALF:], preferred_element_type=F32)
            means = stats[0:count]
            mean = jnp.sum(means, axis=0, keepdims=True) * (1.0 / count)
            off = means - mean
            feats_all = count * group
            var = (
                stats[count : count + 1] + group * jnp.sum(off * off, axis=0, keepdims=True)
            ) / feats_all
            inv = lax.rsqrt(var + EPS)
            shift = lax.dot_general(
                off, table_ref[...], (((0,), (0,)), ((), ())),
                precision=HIGH, preferred_element_type=F32,
            )
            shift = jnp.where(lane40 < 64, shift[0:HALF], shift[64 : 64 + HALF])
            inv_all = jnp.dot(
                jnp.where(spread_mask, inv, 0.0), ones_block,
                precision=HIGH, preferred_element_type=F32,
            )
            halves.append((block[0:HALF].astype(F32) + shift) * inv_all + const_ref[...])
        row = jnp.concatenate(halves, axis=0)
        if j == 0:
            row = jnp.where(has_low > 0, row, 0.0)
        if j == 2:
            row = jnp.where(has_high > 0, row, 0.0)
        swapped = pltpu.roll(row, 64, 1)
        for f in range(2):
            first = lane80 < 64 if f == 0 else lane80 >= 64
            both = pltpu.roll(jnp.where(first, row, swapped), 32, 1)
            before = jnp.where(sub80 == 0, 0.0, pltpu.roll(both, 1, 0))
            after = jnp.where(sub80 == TOK_W - 1, 0.0, pltpu.roll(both, TOK_W - 1, 0))
            edge[f][j] = jnp.where(
                lane80 < 32, before, jnp.where(lane80 >= 96, after, both)
            ).astype(BF)

    def patch(f):
        return jnp.concatenate(
            [jnp.concatenate([edge[f][b], edge[f][b + 1]], axis=1) for b in range(2)], axis=0
        )

    patches = [patch(0), patch(1)]
    bias_in, gain_in = cinv_ref[0:1], cinv_ref[1:2] * 0.5
    sub_one = lax.broadcasted_iota(jnp.int32, (TOK_W, 384), 0)
    zeros_ext = jnp.zeros((TOK_W, 384), F32)
    for f in range(2):
        pre = jnp.dot(patches[f], cin_ref[1], preferred_element_type=F32)
        if f == 1:
            pre = pre + jnp.dot(patches[0], cin_ref[0], preferred_element_type=F32)
        for b in range(2):
            for qy in range(2):
                y = 2 * b + qy
                act = []
                for qx in range(2):
                    col = (qy * 2 + qx) * 384
                    v = pre[b * TOK_W : (b + 1) * TOK_W, col : col + 384] + bias_in
                    mean_sq = jnp.sum(v * v, axis=1, keepdims=True) * (1.0 / 384)
                    a = silu_half(v * lax.rsqrt(mean_sq + EPS) * gain_in)
                    if y == 0:
                        a = jnp.where(has_low > 0, a, 0.0)
                    if y == 3:
                        a = jnp.where(has_high > 0, a, 0.0)
                    act.append(a)
                even, odd = act
                back = jnp.where(sub_one == 0, 0.0, pltpu.roll(odd, 1, 0))
                even, odd, back = even.astype(BF), odd.astype(BF), back.astype(BF)
                for pair, part in ((y - 1, 1), (y, 0)):
                    if not 0 <= pair < 3:
                        continue
                    at = slice((f * 3 + pair) * TOK_W, (f * 3 + pair + 1) * TOK_W)
                    fa[at, part * 768 : part * 768 + 384] = even
                    fa[at, part * 768 + 384 : part * 768 + 768] = odd
                    fb[at, part * 768 : part * 768 + 384] = back
                    fb[at, part * 768 + 384 : part * 768 + 768] = even
                    fx[f * 3 + pair : f * 3 + pair + 1, part * 768 : part * 768 + 384] = act[1][
                        TOK_W - 1 : TOK_W
                    ]
                    fx[f * 3 + pair : f * 3 + pair + 1, part * 768 + 384 : part * 768 + 768] = (
                        zeros_ext[0:1]
                    )
    del sub_one

    def times_up(x):
        dims = (((1,), (1,)), ((), ()))
        return lax.dot_general(x, up_ref[...], dims, preferred_element_type=F32)

    ua[...] = times_up(fa[...])
    ub[0 : 6 * TOK_W] = times_up(fb[...])
    extra_in = jnp.where(
        lax.broadcasted_iota(jnp.int32, (8, 1536), 0) < 6, fx[...], 0.0
    )
    extra_in = jnp.concatenate([extra_in, jnp.zeros((8, 1536), F32)], axis=0).astype(BF)
    extra = times_up(extra_in)[0:8]
    bias_up, gain_up = upv_ref[0:1], upv_ref[1:2] * 0.5

    def second(u):
        v = u + bias_up
        t0, t1, t2 = v[:, 0:128], v[:, 128:256], v[:, 256:384]
        lane = lanes(u.shape[0])
        q = t2 * t2
        left = jnp.sum(t0 * t0 + jnp.where(lane < 64, q, 0.0), axis=1, keepdims=True)
        right = jnp.sum(t1 * t1 + jnp.where(lane < 64, 0.0, q), axis=1, keepdims=True)
        left = lax.rsqrt(left * (1.0 / 192) + EPS)
        right = lax.rsqrt(right * (1.0 / 192) + EPS)
        g = gain_up
        return (
            silu_half(t0 * left * g[:, 0:128]),
            silu_half(t1 * right * g[:, 128:256]),
            silu_half(t2 * jnp.where(lane < 64, left, right) * g[:, 256:384]),
        )

    for f in range(2):
        for pair in range(3):
            at = (f * 3 + pair) * TOK_W
            for py in range(2):
                y = pair * 2 + py
                cols = slice(py * 384, py * 384 + 384)

                def keep(value, y=y):
                    if y == 0:
                        return jnp.where(has_low > 0, value, 0.0)
                    if y == 5:
                        return jnp.where(has_high > 0, value, 0.0)
                    return value

                mid = [keep(t) for t in second(ua[at : at + TOK_W, cols])]
                low = [keep(t) for t in second(ub[at : at + TOK_W, cols])]
                end = [keep(t) for t in second(extra[:, cols])]
                to = slice(y * TOK_W, (y + 1) * TOK_W)
                first = sub80 == 0
                low[0] = jnp.where(first, 0.0, low[0])
                low[2] = jnp.where(first & (lane80 < 64), 0.0, low[2])
                end[1] = jnp.zeros_like(end[1])
                end[2] = jnp.where(lanes(8) < 64, end[2], 0.0)
                for k in range(3):
                    m = mid[k].astype(BF)
                    xe[f, to, k * 128 : k * 128 + 128] = low[k].astype(BF)
                    xe[f, to, 384 + k * 128 : 512 + k * 128] = m
                    xo[f, to, k * 128 : k * 128 + 128] = m
                    last = end[k][f * 3 + pair : f * 3 + pair + 1]
                    ahead = jnp.where(
                        sub80 == TOK_W - 1, last, pltpu.roll(low[k], TOK_W - 1, 0)
                    )
                    xo[f, to, 384 + k * 128 : 512 + k * 128] = ahead.astype(BF)

    bias_out = coutv_ref[...]
    for f in range(2):
        for side, x in enumerate((xe, xo)):
            acc = None
            for b in range(3):
                rows = slice(b * TOK_W, (b + 4) * TOK_W)
                ks = slice(b * 768, b * 768 + 768)
                term = jnp.dot(x[f, rows], cout_ref[1, ks], preferred_element_type=F32)
                acc = term if acc is None else acc + term
                if f == 1:
                    acc = acc + jnp.dot(x[0, rows], cout_ref[0, ks], preferred_element_type=F32)
            for j in range(4):
                for o in range(2):
                    lines[j, pl.ds(2 * side + o, TOK_W, stride=4), :] = (
                        acc[j * TOK_W : (j + 1) * TOK_W, o * 128 : o * 128 + 128] + bias_out
                    )
        for j in range(4):
            out_ref[f, j] = lines[j].T[0:96].astype(BF)


def decode(group, flags, sums, table, const, cin, cinv, up, upv, cout, coutv):
    vmem = pl.BlockSpec(memory_space=pltpu.VMEM)
    return pl.pallas_call(
        functools.partial(decode_kernel, float(group)),
        in_specs=[pl.BlockSpec(memory_space=pltpu.SMEM)] + [vmem] * 9,
        out_specs=vmem,
        out_shape=jax.ShapeDtypeStruct((2, 4, 96, 4 * TOK_W), BF),
        scratch_shapes=[
            pltpu.VMEM((6 * TOK_W, 1536), BF),
            pltpu.VMEM((6 * TOK_W, 1536), BF),
            pltpu.VMEM((8, 1536), F32),
            pltpu.VMEM((6 * TOK_W, 768), F32),
            pltpu.VMEM((6 * TOK_W, 768), F32),
            pltpu.VMEM((2, 6 * TOK_W, 768), BF),
            pltpu.VMEM((2, 6 * TOK_W, 768), BF),
            pltpu.VMEM((4, 4 * TOK_W, 128), F32),
        ],
        compiler_params=pltpu.CompilerParams(vmem_limit_bytes=24 << 20),
        cost_estimate=pl.CostEstimate(
            flops=5_000_000_000, bytes_accessed=8_000_000, transcendentals=1_300_000
        ),
        name="decode",
    )(flags, sums, table, const, cin, cinv, up, upv, cout, coutv)


def exchange(block, mask, count):
    return lax.ppermute(block, "seq", [(i, i ^ mask) for i in range(count)])


def merged(own, received):
    total = own[:, :HALF].astype(F32)
    for item in received:
        total = total + item[:, :HALF].astype(F32)
    return jnp.concatenate(
        [total.astype(BF), own[:, HALF:]] + [item[:, HALF:] for item in received], axis=1
    )


def cut(block, start, size):
    return lax.dynamic_slice_in_dim(block, start, size, 0)


def steps_of(count):
    bit = count.bit_length() - 3
    steps = [[2 << bit, 1 << bit, 3 << bit]]
    while bit > 1:
        bit -= 1
        steps.append([1 << bit])
    return steps


def device_order(count):
    order = [0]
    for masks in steps_of(count):
        order = order + [o ^ mask for mask in masks for o in order]
    return np.asarray([o + c for o in order for c in range(2)], np.int32)


def gather_rows(own, give, weights, ready, me, count):
    core = me & 1
    block = (own.astype(F32) + exchange(give, 1, count).astype(F32)).astype(BF)
    block, weights = lax.optimization_barrier((block, weights))

    def window(base, size):
        return jnp.clip(base - 1, 0, count - size)

    start = jnp.int32(0)
    for masks in steps_of(count):
        unit = min(masks)
        size = unit + 2
        base = (me // unit) * unit
        new = window(base, size)
        received = [
            exchange(cut(block, window(base ^ mask, size) - start, size), mask, count)
            for mask in masks
        ]
        block = merged(cut(block, new - start, size), received)
        if len(masks) > 1:
            block, weights = lax.optimization_barrier((block, ready(weights)))
        start = new
    padded = jnp.pad(block, ((1, 1), (0, 0), (0, 0)))
    mine = cut(padded, me - start, 3)
    other = exchange(cut(padded, (me ^ 1) - start, 3), 1, count)
    low = jnp.where(core == 0, mine, other)
    high = jnp.where(core == 0, other, mine)
    return jnp.stack([low, high]), weights


def local(
    hidden,
    mod_shift,
    mod_scale,
    head_weight,
    head_bias,
    conv_in_weight,
    conv_in_bias,
    gain_in,
    up_weight,
    up_bias,
    gain_up,
    out_weight,
    out_bias,
):
    count = lax.axis_size("seq")
    me = lax.axis_index("seq")
    feats = hidden.shape[1]
    flags = jnp.stack([me, (me > 0).astype(jnp.int32), (me < count - 1).astype(jnp.int32)])
    own, give = project(flags, hidden, head_weight, mod_scale[None])
    weights = (head_weight, conv_in_weight, jnp.swapaxes(up_weight, 2, 3), out_weight)

    def ready(parts):
        head_again, cin, up, cout = parts
        return prepare(
            head_again, mod_scale[None], mod_shift[None], head_bias[None],
            (((me // 2) * 2) ^ device_order(count))[:, None],
            cin, up, jnp.stack([up_bias, gain_up]), cout,
        )

    sums, weights = gather_rows(own, give, weights, ready, me, count)
    table, const, cin, up, upv, cout = weights
    cinv = jnp.stack([conv_in_bias, gain_in])
    coutv = jnp.pad(out_bias, (0, 32))[None]
    out = decode(feats, flags, sums, table, const, cin, cinv, up, upv, cout, coutv)
    return jnp.swapaxes(out, 2, 3)


def solution(mesh):
    placed = (P("grp", "seq", None), P(), P(), P(), P(), P(), P(), P(), P(), P(), P(), P(), P())
    return jax.shard_map(
        local, mesh=mesh, in_specs=placed, out_specs=P("grp", "seq", None, None), check_vma=False
    )
```

```python
import functools
import jax
import jax.numpy as jnp
import numpy as np
from jax import lax
from jax.experimental import pallas as pl
from jax.experimental.pallas import tpu as pltpu
from jax.sharding import PartitionSpec as P

TOK_W = 80
HALF = TOK_W // 2
STAT = 4
EPS = 1e-06
HIGH = lax.Precision.HIGHEST
BF = jnp.bfloat16
F32 = jnp.float32


def in_hbm(value):
    return pltpu.with_memory_space_constraint(value, pltpu.HBM)


def split(values):
    high = values.astype(BF).astype(F32)
    return high, values - high


def lanes(rows):
    return lax.broadcasted_iota(jnp.int32, (rows, 128), 1)


def project_kernel(flags_ref, hid_ref, w_ref, scale_ref, own_ref, give_ref, hid, w, scale, sems):
    frames, feats, tokens = hid_ref.shape
    width = hid.shape[3]
    me = flags_ref[0]
    core = me & 1
    wide = w.shape[1]
    at = jnp.minimum(lax.div(me * feats, 128) * 128, w_ref.shape[1] - wide)
    at = pl.multiple_of(at, 128)
    copies = [
        pltpu.make_async_copy(w_ref.at[:, pl.ds(at, wide)], w, sems.at[0]),
        pltpu.make_async_copy(scale_ref.at[:, pl.ds(at, wide)], scale, sems.at[1]),
    ]
    blocks = tokens // width
    for i in range(blocks):
        copies.append(
            pltpu.make_async_copy(
                hid_ref.at[:, :, pl.ds(i * width, width)], hid.at[i], sems.at[2 + i]
            )
        )
    for copy in copies:
        copy.start()
    copies[0].wait()
    copies[1].wait()
    gain = w[...] * (1.0 + scale[...])
    gain = pltpu.roll(gain, wide - (me * feats - at), 1)[:, :feats]
    gain = jnp.concatenate([gain[0:16], gain[32:48], gain[16:32], gain[48:64]], axis=0)
    high, low = split(gain)
    gain_sum = jnp.sum(gain, axis=1, keepdims=True)
    stack = jnp.concatenate([high, low, jnp.ones((16, feats), F32)], axis=0).astype(BF)
    lane = lanes(8)
    sub = lax.broadcasted_iota(jnp.int32, (8, 128), 0)
    for i in range(blocks):
        copies[2 + i].wait()
        parts, stats = [], []
        for f in range(frames):
            x = hid[i, f]
            prod = jnp.dot(stack, x, preferred_element_type=F32)
            mean = prod[128:129] * (1.0 / feats)
            parts.append(prod[0:64] + prod[64:128] - gain_sum * mean)
            off = x.astype(F32) - mean
            second = jnp.sum(off * off, axis=0, keepdims=True)
            m_hi, m_lo = split(mean)
            s_hi, s_lo = split(second)
            four = jnp.concatenate([m_hi, m_lo, s_hi, s_lo] * 2, axis=0)
            stats.append(four)
        flat = jnp.concatenate(parts, axis=0).T
        for row in range(width // TOK_W):
            pair = []
            for h in range(2):
                first = row * TOK_W + h * HALF
                base = (first // 128) * 128
                span = min(256, width - base)
                picks = []
                for f in range(2):
                    window = stats[f][:, base : base + span]
                    shift = (64 * f - (first - base)) % span
                    if shift:
                        window = pltpu.roll(window, shift, 1)
                    picks.append(window[:, :128])
                tail = jnp.where(
                    lane < HALF,
                    picks[0],
                    jnp.where((lane >= 64) & (lane < 64 + HALF), picks[1], 0.0),
                )
                tail = jnp.where(lax.div(sub, STAT) == core, tail, 0.0)
                pair.append(jnp.concatenate([flat[first : first + HALF], tail], axis=0))
            to = i * (width // TOK_W) + row
            own_ref[to] = jnp.where(core == 0, pair[0], pair[1]).astype(BF)
            give_ref[to] = jnp.where(core == 0, pair[1], pair[0]).astype(BF)


def project(flags, hidden, head_weight, scale):
    frames, feats, tokens = hidden.shape
    width = 640
    rows = tokens // TOK_W
    wide = min(head_weight.shape[1], (feats + 127) // 128 * 128 + 128)
    hbm = pl.BlockSpec(memory_space=pltpu.HBM)
    vmem = pl.BlockSpec(memory_space=pltpu.VMEM)
    return pl.pallas_call(
        project_kernel,
        in_specs=[pl.BlockSpec(memory_space=pltpu.SMEM), hbm, hbm, hbm],
        out_specs=[vmem, vmem],
        out_shape=[jax.ShapeDtypeStruct((rows, HALF + 2 * STAT, 128), BF)] * 2,
        scratch_shapes=[
            pltpu.VMEM((tokens // width, frames, feats, width), BF),
            pltpu.VMEM((64, wide), F32),
            pltpu.VMEM((1, wide), F32),
            pltpu.SemaphoreType.DMA((2 + tokens // width,)),
        ],
        compiler_params=pltpu.CompilerParams(vmem_limit_bytes=16 << 20),
        name="project",
    )(flags, in_hbm(hidden), in_hbm(head_weight), in_hbm(scale))


def prepare_first(cin_ref, cin_out):
    zero16 = jnp.zeros((16, 384), BF)
    for tap in range(2):
        for ly in range(4):
            for lx in range(4):
                row = (ly // 2) * 128 + lx * 32 + (ly % 2) * 16
                for qy in range(2):
                    for qx in range(2):
                        dy, dx = ly - qy, lx - qx
                        good = 0 <= dy < 3 and 0 <= dx < 3
                        piece = cin_ref[tap + 1, dy, dx] if good else zero16
                        col = (qy * 2 + qx) * 384
                        cin_out[tap, row : row + 16, col : col + 384] = piece


def prepare_up(up_ref, up_out):
    taps = {(0, 0): (0, 1), (0, 1): (2,), (1, 0): (0,), (1, 1): (1, 2)}
    for dx in range(2):
        for dy in range(2):
            for py in range(2):
                for px in range(2):
                    total = None
                    for b in taps[py, dy]:
                        for e in taps[px, dx]:
                            term = up_ref[b, e].astype(F32)
                            total = term if total is None else total + term
                    total = total.astype(BF)
                    k = slice((dy * 2 + dx) * 384, (dy * 2 + dx + 1) * 384)
                    n = py * 384
                    up_out[n + px * 128 : n + px * 128 + 128, k] = total[0:128]
                    up_out[n + 256 + px * 64 : n + 320 + px * 64, k] = total[128:192]


def prepare_last(cout_ref, cout_out):
    cout_out[...] = jnp.zeros(cout_out.shape, BF)
    for tap in range(2):
        for b in range(3):
            for v in range(2):
                for s in range(2):
                    for o in range(2):
                        e = 2 * v + s - o
                        if not 0 <= e < 3:
                            continue
                        row = b * 768 + v * 384
                        weight = cout_ref[tap + 1, b, e]
                        lo = row + s * 128
                        hi = row + 256 + s * 64
                        cout_out[tap, lo : lo + 128, o * 128 : o * 128 + 96] = weight[0:128]
                        cout_out[tap, hi : hi + 64, o * 128 : o * 128 + 96] = weight[128:192]


def prepare_kernel(
    w_ref, scale_ref, shift_ref, hb_ref, dev_ref, cin_ref, up_ref, upv_ref, cout_ref,
    table_ref, const_ref, cin_out, up_out, upv_out, cout_out, w, cin, up, cout, sems,
):
    copies = [
        pltpu.make_async_copy(source, target, sems.at[i])
        for i, (source, target) in enumerate(
            ((cin_ref, cin), (up_ref, up), (cout_ref, cout), (w_ref, w))
        )
    ]
    for copy in copies:
        copy.start()
    copies[0].wait()
    prepare_first(cin, cin_out)
    copies[1].wait()
    prepare_up(up, up_out)
    vec = upv_ref[...]
    upv_out[...] = jnp.concatenate(
        [vec[:, 0:128], vec[:, 0:128], vec[:, 128:192], vec[:, 128:192]], axis=1
    )
    copies[2].wait()
    prepare_last(cout, cout_out)
    copies[3].wait()
    feats = w_ref.shape[1] // dev_ref.shape[0]
    head = w[...]
    head = jnp.concatenate([head[0:16], head[32:48], head[16:32], head[48:64]], axis=0)
    gain = head * (1.0 + scale_ref[...])
    count = dev_ref.shape[0]
    place = lax.broadcasted_iota(jnp.int32, (count, w_ref.shape[1]), 1) - dev_ref[...] * feats
    inside = ((place >= 0) & (place < feats)).astype(F32)
    dims = (((1,), (1,)), ((), ()))
    sums = lax.dot_general(inside, gain, dims, precision=HIGH, preferred_element_type=F32)
    table_ref[...] = jnp.concatenate([sums, sums], axis=1)
    const = lax.dot_general(
        shift_ref[...], head, dims, precision=HIGH, preferred_element_type=F32
    )
    hb = hb_ref[...]
    hb = jnp.concatenate([hb[:, 0:16], hb[:, 32:48], hb[:, 16:32], hb[:, 48:64]], axis=1)
    const = const + hb
    const_ref[...] = jnp.concatenate([const, const], axis=1)


def prepare(head_weight, mod_scale, mod_shift, head_bias, devs, cin, up, upv, cout):
    count = devs.shape[0]
    hbm = pl.BlockSpec(memory_space=pltpu.HBM)
    vmem = pl.BlockSpec(memory_space=pltpu.VMEM)
    return pl.pallas_call(
        prepare_kernel,
        in_specs=[hbm, vmem, vmem, vmem, vmem, hbm, hbm, vmem, hbm],
        scratch_shapes=[
            pltpu.VMEM(head_weight.shape, F32),
            pltpu.VMEM(cin.shape, BF),
            pltpu.VMEM(up.shape, BF),
            pltpu.VMEM(cout.shape, BF),
            pltpu.SemaphoreType.DMA((4,)),
        ],
        out_shape=[
            jax.ShapeDtypeStruct((count, 128), F32),
            jax.ShapeDtypeStruct((1, 128), F32),
            jax.ShapeDtypeStruct((2, 256, 1536), BF),
            jax.ShapeDtypeStruct((768, 1536), BF),
            jax.ShapeDtypeStruct((2, 384), F32),
            jax.ShapeDtypeStruct((2, 2304, 256), BF),
        ],
        compiler_params=pltpu.CompilerParams(vmem_limit_bytes=20 << 20),
        cost_estimate=pl.CostEstimate(
            flops=20_000_000, bytes_accessed=10_000_000, transcendentals=0
        ),
        name="prepare",
    )(
        in_hbm(head_weight), mod_scale, mod_shift, head_bias, devs, in_hbm(cin), in_hbm(up), upv,
        in_hbm(cout),
    )


def silu_half(half):
    return half + half * jnp.tanh(half)


def decode_kernel(
    group, flags_ref, own_ref, near_ref, core_ref, far_ref, table_ref, const_ref, cin_ref, cinv_ref, up_ref, upv_ref, cout_ref,
    coutv_ref, out_ref, fa, fb, fx, ua, ub, xe, xo, lines, outs, sems,
):
    count = table_ref.shape[0]
    has_low = flags_ref[1]
    has_high = flags_ref[2]
    n_stat = 2 * (own_ref.shape[1] - HALF)
    first_half = (flags_ref[0] & 1) == 0

    pick_row = lax.broadcasted_iota(jnp.int32, (count + 8, n_stat), 0)
    pick_col = lax.broadcasted_iota(jnp.int32, (count + 8, n_stat), 1)
    of_dev, of_kind = pick_col // STAT, pick_col % STAT
    pick = ((of_kind < 2) & (pick_row == of_dev)) | ((of_kind >= 2) & (pick_row == count))
    pick = pick.astype(F32).astype(BF)
    lane40 = lanes(HALF)
    lane80, sub80 = lanes(TOK_W), lax.broadcasted_iota(jnp.int32, (TOK_W, 128), 0)
    wide = []
    for j in range(3):
        mine, other = [
            jnp.concatenate([a[j, HALF:], b[j, HALF:]], axis=0)
            for a, b in ((own_ref, near_ref), (core_ref, far_ref))
        ]
        wide += [jnp.where(first_half, mine, other), jnp.where(first_half, other, mine)]
    wide = jnp.concatenate(wide, axis=1)
    stats = jnp.dot(pick, wide, preferred_element_type=F32)
    means = stats[0:count]
    off = means - jnp.sum(means, axis=0, keepdims=True) * (1.0 / count)
    var = stats[count : count + 1] + group * jnp.sum(off * off, axis=0, keepdims=True)
    inv = lax.rsqrt(var * (1.0 / (count * group)) + EPS)
    off_hi, off_lo = split(off)
    inv_hi, inv_lo = split(inv)
    left = jnp.concatenate(
        [off_hi, off_lo, off_hi, inv_hi, inv_lo, jnp.zeros((14, off.shape[1]), F32)], axis=0
    )
    tab_hi, tab_lo = split(table_ref[...])
    right = jnp.concatenate(
        [
            jnp.concatenate([tab_hi, tab_hi, tab_lo, jnp.zeros((16, 128), F32)], axis=0),
            jnp.concatenate(
                [
                    jnp.zeros((3 * count, 128), F32),
                    jnp.ones((2, 128), F32),
                    jnp.zeros((14, 128), F32),
                ],
                axis=0,
            ),
        ],
        axis=1,
    )
    per_token = jnp.dot(left.T.astype(BF), right.astype(BF), preferred_element_type=F32)
    edge = [[None] * 3 for _ in range(2)]
    for j in range(3):
        halves = []
        mine, other = [
            a[j, 0:HALF].astype(F32) + b[j, 0:HALF].astype(F32)
            for a, b in ((own_ref, near_ref), (core_ref, far_ref))
        ]
        sums = [jnp.where(first_half, mine, other), jnp.where(first_half, other, mine)]
        for h in range(2):
            at = (j * 2 + h) * 128
            both = jnp.concatenate([lane40, lane40], axis=1) % 128 < 64
            token = jnp.where(both, per_token[at : at + HALF], per_token[at + 64 : at + 64 + HALF])
            halves.append(
                (sums[h] + token[:, 0:128]) * token[:, 128:256]
                + const_ref[...]
            )
        row = jnp.concatenate(halves, axis=0)
        if j == 0:
            row = jnp.where(has_low > 0, row, 0.0)
        if j == 2:
            row = jnp.where(has_high > 0, row, 0.0)
        swapped = pltpu.roll(row, 64, 1)
        for f in range(2):
            first = lane80 < 64 if f == 0 else lane80 >= 64
            both = pltpu.roll(jnp.where(first, row, swapped), 32, 1)
            before = jnp.where(sub80 == 0, 0.0, pltpu.roll(both, 1, 0))
            after = jnp.where(sub80 == TOK_W - 1, 0.0, pltpu.roll(both, TOK_W - 1, 0))
            edge[f][j] = jnp.where(
                lane80 < 32, before, jnp.where(lane80 >= 96, after, both)
            ).astype(BF)

    def patch(f):
        return jnp.concatenate(
            [jnp.concatenate([edge[f][b], edge[f][b + 1]], axis=1) for b in range(2)], axis=0
        )

    patches = [patch(0), patch(1)]
    bias_in, gain_in = cinv_ref[0:1], cinv_ref[1:2] * 0.5
    sub_one = lax.broadcasted_iota(jnp.int32, (TOK_W, 384), 0)
    zeros_ext = jnp.zeros((TOK_W, 384), F32)
    for f in range(2):
        pre = jnp.dot(patches[f], cin_ref[1], preferred_element_type=F32)
        if f == 1:
            pre = pre + jnp.dot(patches[0], cin_ref[0], preferred_element_type=F32)
        for b in range(2):
            for qy in range(2):
                y = 2 * b + qy
                act = []
                for qx in range(2):
                    col = (qy * 2 + qx) * 384
                    v = pre[b * TOK_W : (b + 1) * TOK_W, col : col + 384] + bias_in
                    mean_sq = jnp.sum(v * v, axis=1, keepdims=True) * (1.0 / 384)
                    a = silu_half(v * lax.rsqrt(mean_sq + EPS) * gain_in)
                    if y == 0:
                        a = jnp.where(has_low > 0, a, 0.0)
                    if y == 3:
                        a = jnp.where(has_high > 0, a, 0.0)
                    act.append(a)
                even, odd = act
                back = jnp.where(sub_one == 0, 0.0, pltpu.roll(odd, 1, 0))
                even, odd, back = even.astype(BF), odd.astype(BF), back.astype(BF)
                for pair, part in ((y - 1, 1), (y, 0)):
                    if not 0 <= pair < 3:
                        continue
                    at = slice((f * 3 + pair) * TOK_W, (f * 3 + pair + 1) * TOK_W)
                    fa[at, part * 768 : part * 768 + 384] = even
                    fa[at, part * 768 + 384 : part * 768 + 768] = odd
                    fb[at, part * 768 : part * 768 + 384] = back
                    fb[at, part * 768 + 384 : part * 768 + 768] = even
                    fx[f * 3 + pair : f * 3 + pair + 1, part * 768 : part * 768 + 384] = act[1][
                        TOK_W - 1 : TOK_W
                    ]
                    fx[f * 3 + pair : f * 3 + pair + 1, part * 768 + 384 : part * 768 + 768] = (
                        zeros_ext[0:1]
                    )
    del sub_one

    def times_up(x):
        dims = (((1,), (1,)), ((), ()))
        return lax.dot_general(x, up_ref[...], dims, preferred_element_type=F32)

    ua[...] = times_up(fa[...])
    extra_in = jnp.where(
        lax.broadcasted_iota(jnp.int32, (8, 1536), 0) < 6, fx[...], 0.0
    )
    extra_in = jnp.concatenate([extra_in, jnp.zeros((8, 1536), F32)], axis=0).astype(BF)
    fb[6 * TOK_W :] = extra_in
    ub[...] = times_up(fb[...])
    extra = ub[6 * TOK_W : 6 * TOK_W + 8]
    bias_up, gain_up = upv_ref[0:1], upv_ref[1:2] * 0.5

    def second(u):
        v = u + bias_up
        t0, t1, t2 = v[:, 0:128], v[:, 128:256], v[:, 256:384]
        lane = lanes(u.shape[0])
        q = t2 * t2
        left = jnp.sum(t0 * t0 + jnp.where(lane < 64, q, 0.0), axis=1, keepdims=True)
        right = jnp.sum(t1 * t1 + jnp.where(lane < 64, 0.0, q), axis=1, keepdims=True)
        left = lax.rsqrt(left * (1.0 / 192) + EPS)
        right = lax.rsqrt(right * (1.0 / 192) + EPS)
        g = gain_up
        return (
            silu_half(t0 * left * g[:, 0:128]),
            silu_half(t1 * right * g[:, 128:256]),
            silu_half(t2 * jnp.where(lane < 64, left, right) * g[:, 256:384]),
        )

    for f in range(2):
        for pair in range(3):
            at = (f * 3 + pair) * TOK_W
            for py in range(2):
                y = pair * 2 + py
                cols = slice(py * 384, py * 384 + 384)

                def keep(value, y=y):
                    if y == 0:
                        return jnp.where(has_low > 0, value, 0.0)
                    if y == 5:
                        return jnp.where(has_high > 0, value, 0.0)
                    return value

                mid = [keep(t) for t in second(ua[at : at + TOK_W, cols])]
                low = [keep(t) for t in second(ub[at : at + TOK_W, cols])]
                end = [keep(t) for t in second(extra[:, cols])]
                to = slice(y * TOK_W, (y + 1) * TOK_W)
                first = sub80 == 0
                low[0] = jnp.where(first, 0.0, low[0])
                low[2] = jnp.where(first & (lane80 < 64), 0.0, low[2])
                end[1] = jnp.zeros_like(end[1])
                end[2] = jnp.where(lanes(8) < 64, end[2], 0.0)
                for k in range(3):
                    m = mid[k].astype(BF)
                    xe[f, to, k * 128 : k * 128 + 128] = low[k].astype(BF)
                    xe[f, to, 384 + k * 128 : 512 + k * 128] = m
                    xo[f, to, k * 128 : k * 128 + 128] = m
                    last = end[k][f * 3 + pair : f * 3 + pair + 1]
                    ahead = jnp.where(
                        sub80 == TOK_W - 1, last, pltpu.roll(low[k], TOK_W - 1, 0)
                    )
                    xo[f, to, 384 + k * 128 : 512 + k * 128] = ahead.astype(BF)

    bias_out = coutv_ref[...]
    copies = []
    for f in range(2):
        for side, x in enumerate((xe, xo)):
            acc = None
            for b in range(3):
                rows = slice(b * TOK_W, (b + 4) * TOK_W)
                ks = slice(b * 768, b * 768 + 768)
                term = jnp.dot(x[f, rows], cout_ref[1, ks], preferred_element_type=F32)
                acc = term if acc is None else acc + term
                if f == 1:
                    acc = acc + jnp.dot(x[0, rows], cout_ref[0, ks], preferred_element_type=F32)
            for j in range(4):
                for o in range(2):
                    lines[f, j, pl.ds(2 * side + o, TOK_W, stride=4), :] = (
                        acc[j * TOK_W : (j + 1) * TOK_W, o * 128 : o * 128 + 128] + bias_out
                    )
        for j in range(4):
            outs[f, j] = lines[f, j].T[0:96].astype(BF)
        copy = pltpu.make_async_copy(outs.at[f], out_ref.at[f], sems.at[f])
        copy.start()
        copies.append(copy)
    for copy in copies:
        copy.wait()


def decode(group, flags, pieces, table, const, cin, cinv, up, upv, cout, coutv):
    vmem = pl.BlockSpec(memory_space=pltpu.VMEM)
    return pl.pallas_call(
        functools.partial(decode_kernel, float(group)),
        in_specs=[pl.BlockSpec(memory_space=pltpu.SMEM)] + [vmem] * 12,
        out_specs=pl.BlockSpec(memory_space=pltpu.HBM),
        out_shape=jax.ShapeDtypeStruct((2, 4, 96, 4 * TOK_W), BF),
        scratch_shapes=[
            pltpu.VMEM((6 * TOK_W, 1536), BF),
            pltpu.VMEM((6 * TOK_W + 16, 1536), BF),
            pltpu.VMEM((8, 1536), F32),
            pltpu.VMEM((6 * TOK_W, 768), F32),
            pltpu.VMEM((6 * TOK_W + 16, 768), F32),
            pltpu.VMEM((2, 6 * TOK_W, 768), BF),
            pltpu.VMEM((2, 6 * TOK_W, 768), BF),
            pltpu.VMEM((2, 4, 4 * TOK_W, 128), F32),
            pltpu.VMEM((2, 4, 96, 4 * TOK_W), BF),
            pltpu.SemaphoreType.DMA((2,)),
        ],
        compiler_params=pltpu.CompilerParams(vmem_limit_bytes=24 << 20),
        cost_estimate=pl.CostEstimate(
            flops=5_000_000_000, bytes_accessed=8_000_000, transcendentals=1_300_000
        ),
        name="decode",
    )(flags, *pieces, table, const, cin, cinv, up, upv, cout, coutv)


def exchange(block, mask, count):
    return lax.ppermute(block, "seq", [(i, i ^ mask) for i in range(count)])


def merged(own, received):
    total = own[:, :HALF].astype(F32)
    for item in received:
        total = total + item[:, :HALF].astype(F32)
    return jnp.concatenate(
        [total.astype(BF), own[:, HALF:]] + [item[:, HALF:] for item in received], axis=1
    )


def cut(block, start, size):
    return lax.dynamic_slice_in_dim(block, start, size, 0)


def steps_of(count):
    bit = count.bit_length() - 3
    steps = [[2 << bit, 1 << bit, 3 << bit]]
    while bit > 2:
        bit -= 1
        steps.append([1 << bit])
    return steps


def device_order(count):
    order = [0]
    for masks in steps_of(count):
        order = order + [o ^ mask for mask in masks for o in order]
    order = order + [o ^ 2 for o in order]
    return np.asarray([o + c for o in order for c in range(2)], np.int32)


def gather_rows(own, give, weights, ready, me, count):
    block = (own.astype(F32) + exchange(give, 1, count).astype(F32)).astype(BF)
    block, weights = lax.optimization_barrier((block, weights))

    def window(base, size):
        return jnp.clip(base - 1, 0, count - size)

    start = jnp.int32(0)
    for masks in steps_of(count):
        unit = min(masks)
        size = unit + 2
        base = (me // unit) * unit
        new = window(base, size)
        received = [
            exchange(cut(block, window(base ^ mask, size) - start, size), mask, count)
            for mask in masks
        ]
        block = merged(cut(block, new - start, size), received)
        if len(masks) > 1:
            block, weights = lax.optimization_barrier((block, ready(weights)))
        start = new
    padded = jnp.pad(block, ((1, 1), (0, 0), (0, 0)))
    pieces = [cut(padded, me - start, 3)]
    for mask in (2, 1, 3):
        pieces.append(exchange(cut(padded, (me ^ mask) - start, 3), mask, count))
    return pieces, weights


def local(
    hidden,
    mod_shift,
    mod_scale,
    head_weight,
    head_bias,
    conv_in_weight,
    conv_in_bias,
    gain_in,
    up_weight,
    up_bias,
    gain_up,
    out_weight,
    out_bias,
):
    count = lax.axis_size("seq")
    me = lax.axis_index("seq")
    feats = hidden.shape[1]
    flags = jnp.stack([me, (me > 0).astype(jnp.int32), (me < count - 1).astype(jnp.int32)])
    own, give = project(flags, hidden, head_weight, mod_scale[None])
    weights = (head_weight, conv_in_weight, jnp.swapaxes(up_weight, 2, 3), out_weight)

    def ready(parts):
        head_again, cin, up, cout = parts
        return prepare(
            head_again, mod_scale[None], mod_shift[None], head_bias[None],
            (((me // 2) * 2) ^ device_order(count))[:, None],
            cin, up, jnp.stack([up_bias, gain_up]), cout,
        )

    pieces, weights = gather_rows(own, give, weights, ready, me, count)
    table, const, cin, up, upv, cout = weights
    cinv = jnp.stack([conv_in_bias, gain_in])
    coutv = jnp.pad(out_bias, (0, 32))[None]
    out = decode(feats, flags, pieces, table, const, cin, cinv, up, upv, cout, coutv)
    return jnp.swapaxes(out, 2, 3)


def solution(mesh):
    placed = (P("grp", "seq", None), P(), P(), P(), P(), P(), P(), P(), P(), P(), P(), P(), P())
    return jax.shard_map(
        local, mesh=mesh, in_specs=placed, out_specs=P("grp", "seq", None, None), check_vma=False
    )
```

```python
import functools
import jax
import jax.numpy as jnp
import numpy as np
from jax import lax
from jax.experimental import pallas as pl
from jax.experimental.pallas import tpu as pltpu
from jax.sharding import PartitionSpec as P

TOK_W = 80
HALF = TOK_W // 2
STAT = 4
EPS = 1e-06
HIGH = lax.Precision.HIGHEST
BF = jnp.bfloat16
F32 = jnp.float32


def in_hbm(value):
    return pltpu.with_memory_space_constraint(value, pltpu.HBM)


def split(values):
    high = values.astype(BF).astype(F32)
    return high, values - high


def lanes(rows):
    return lax.broadcasted_iota(jnp.int32, (rows, 128), 1)


def frame_sums(x, stack, gain_sum, core, out_ref):
    feats, tokens = x.shape
    width = 640
    lane40 = lanes(HALF)
    lane = lanes(8)
    sub = lax.broadcasted_iota(jnp.int32, (8, 128), 0)
    for i in range(tokens // width):
        block = x[:, i * width : (i + 1) * width]
        prod = jnp.dot(stack, block, preferred_element_type=F32)
        mean = prod[128:129] * (1.0 / feats)
        part = prod[0:64] + prod[64:128] - gain_sum * mean
        off = block.astype(F32) - mean
        second = jnp.sum(off * off, axis=0, keepdims=True)
        m_hi, m_lo = split(mean)
        s_hi, s_lo = split(second)
        stats = jnp.concatenate([m_hi, m_lo, s_hi, s_lo] * 2, axis=0)
        flat = jnp.concatenate([part, part], axis=0).T
        for row in range(width // TOK_W):
            first = row * TOK_W
            sums = jnp.where(
                lane40 < 64, flat[first : first + HALF], flat[first + HALF : first + TOK_W]
            )
            picks = []
            for h in range(2):
                at = first + h * HALF
                base = (at // 128) * 128
                span = min(256, width - base)
                window = stats[:, base : base + span]
                shift = (64 * h - (at - base)) % span
                if shift:
                    window = pltpu.roll(window, shift, 1)
                picks.append(window[:, :128])
            tail = jnp.where(
                lane < HALF,
                picks[0],
                jnp.where((lane >= 64) & (lane < 64 + HALF), picks[1], 0.0),
            )
            tail = jnp.where(lax.div(sub, STAT) == core, tail, 0.0)
            out_ref[i * (width // TOK_W) + row] = jnp.concatenate([sums, tail], axis=0).astype(BF)


def project_give_kernel(
    hid_ref, w_ref, scale_ref, give_ref, own_ref, stack_ref, gsum_ref,
    hid, w, scale, sems,
):
    feats = hid_ref.shape[1]
    me = lax.axis_index("seq")
    core = me & 1
    wide = w.shape[1]
    at = jnp.minimum(lax.div(me * feats, 128) * 128, w_ref.shape[1] - wide)
    at = pl.multiple_of(at, 128)
    copies = [
        pltpu.make_async_copy(w_ref.at[:, pl.ds(at, wide)], w, sems.at[0]),
        pltpu.make_async_copy(scale_ref.at[:, pl.ds(at, wide)], scale, sems.at[1]),
        pltpu.make_async_copy(hid_ref.at[1 - core], hid, sems.at[2]),
        pltpu.make_async_copy(hid_ref.at[core], own_ref, sems.at[3]),
    ]
    for copy in copies:
        copy.start()
    copies[0].wait()
    copies[1].wait()
    gain = w[...] * (1.0 + scale[...])
    gain = pltpu.roll(gain, wide - (me * feats - at), 1)[:, :feats]
    gain = jnp.concatenate([gain[0:16], gain[32:48], gain[16:32], gain[48:64]], axis=0)
    high, low = split(gain)
    gain_sum = jnp.sum(gain, axis=1, keepdims=True)
    stack = jnp.concatenate([high, low, jnp.ones((16, feats), F32)], axis=0).astype(BF)
    stack_ref[...] = stack
    gsum_ref[...] = jnp.broadcast_to(gain_sum, gsum_ref.shape)
    copies[2].wait()
    frame_sums(hid[...], stack, gain_sum, core, give_ref)
    copies[3].wait()


def project_own_kernel(hid_ref, stack_ref, gsum_ref, own_ref):
    frame_sums(
        hid_ref[...], stack_ref[...], gsum_ref[:, 0:1], lax.axis_index("seq") & 1, own_ref
    )


def project(hidden, head_weight, scale):
    _, feats, tokens = hidden.shape
    rows = tokens // TOK_W
    wide = min(head_weight.shape[1], (feats + 127) // 128 * 128 + 128)
    hbm = pl.BlockSpec(memory_space=pltpu.HBM)
    vmem = pl.BlockSpec(memory_space=pltpu.VMEM)
    sums = jax.ShapeDtypeStruct((rows, HALF + 2 * STAT, 128), BF)
    params = pltpu.CompilerParams(vmem_limit_bytes=16 << 20)
    give, frame, stack, gsum = pl.pallas_call(
        project_give_kernel,
        in_specs=[hbm, hbm, hbm],
        out_specs=[vmem] * 4,
        out_shape=[
            sums,
            jax.ShapeDtypeStruct((feats, tokens), BF),
            jax.ShapeDtypeStruct((144, feats), BF),
            jax.ShapeDtypeStruct((64, 128), F32),
        ],
        scratch_shapes=[
            pltpu.VMEM((feats, tokens), BF),
            pltpu.VMEM((64, wide), F32),
            pltpu.VMEM((1, wide), F32),
            pltpu.SemaphoreType.DMA((4,)),
        ],
        compiler_params=params,
        name="project_give",
    )(in_hbm(hidden), in_hbm(head_weight), in_hbm(scale))

    own = pl.pallas_call(
        project_own_kernel,
        in_specs=[vmem, vmem, vmem],
        out_specs=vmem,
        out_shape=sums,
        compiler_params=params,
        cost_estimate=pl.CostEstimate(
            flops=2 * 144 * feats * tokens, bytes_accessed=1_300_000, transcendentals=0
        ),
        name="project_own",
    )(frame, stack, gsum)
    return own, give


def prepare_first(cin_ref, cin_out):
    zero16 = jnp.zeros((16, 384), BF)
    for tap in range(2):
        for ly in range(4):
            for lx in range(4):
                row = (ly // 2) * 128 + lx * 32 + (ly % 2) * 16
                for qy in range(2):
                    for qx in range(2):
                        dy, dx = ly - qy, lx - qx
                        good = 0 <= dy < 3 and 0 <= dx < 3
                        piece = cin_ref[tap + 1, dy, dx] if good else zero16
                        col = (qy * 2 + qx) * 384
                        cin_out[tap, row : row + 16, col : col + 384] = piece


def prepare_up(up_ref, up_out):
    taps = {(0, 0): (0, 1), (0, 1): (2,), (1, 0): (0,), (1, 1): (1, 2)}
    for dx in range(2):
        for dy in range(2):
            for py in range(2):
                for px in range(2):
                    total = None
                    for b in taps[py, dy]:
                        for e in taps[px, dx]:
                            term = up_ref[b, e].astype(F32)
                            total = term if total is None else total + term
                    total = total.astype(BF)
                    k = slice((dy * 2 + dx) * 384, (dy * 2 + dx + 1) * 384)
                    n = py * 384
                    up_out[n + px * 128 : n + px * 128 + 128, k] = total[0:128]
                    up_out[n + 256 + px * 64 : n + 320 + px * 64, k] = total[128:192]


def prepare_last(cout_ref, cout_out):
    cout_out[...] = jnp.zeros(cout_out.shape, BF)
    for tap in range(2):
        for b in range(3):
            for v in range(2):
                for s in range(2):
                    for o in range(2):
                        e = 2 * v + s - o
                        if not 0 <= e < 3:
                            continue
                        row = b * 768 + v * 384
                        weight = cout_ref[tap + 1, b, e]
                        lo = row + s * 128
                        hi = row + 256 + s * 64
                        cout_out[tap, lo : lo + 128, o * 128 : o * 128 + 96] = weight[0:128]
                        cout_out[tap, hi : hi + 64, o * 128 : o * 128 + 96] = weight[128:192]


def prepare_kernel(
    w_ref, scale_ref, shift_ref, hb_ref, dev_ref, cin_ref, up_ref, upv_ref, cout_ref,
    table_ref, const_ref, cin_out, up_out, upv_out, cout_out, w, cin, up, cout, sems,
):
    copies = [
        pltpu.make_async_copy(source, target, sems.at[i])
        for i, (source, target) in enumerate(
            ((cin_ref, cin), (up_ref, up), (cout_ref, cout), (w_ref, w))
        )
    ]
    for copy in copies:
        copy.start()
    copies[0].wait()
    prepare_first(cin, cin_out)
    copies[1].wait()
    prepare_up(up, up_out)
    vec = upv_ref[...]
    upv_out[...] = jnp.concatenate(
        [vec[:, 0:128], vec[:, 0:128], vec[:, 128:192], vec[:, 128:192]], axis=1
    )
    copies[2].wait()
    prepare_last(cout, cout_out)
    copies[3].wait()
    feats = w_ref.shape[1] // dev_ref.shape[0]
    head = w[...]
    head = jnp.concatenate([head[0:16], head[32:48], head[16:32], head[48:64]], axis=0)
    gain = head * (1.0 + scale_ref[...])
    count = dev_ref.shape[0]
    place = lax.broadcasted_iota(jnp.int32, (count, w_ref.shape[1]), 1) - dev_ref[...] * feats
    inside = ((place >= 0) & (place < feats)).astype(F32)
    dims = (((1,), (1,)), ((), ()))
    sums = lax.dot_general(inside, gain, dims, precision=HIGH, preferred_element_type=F32)
    table_ref[...] = jnp.concatenate([sums, sums], axis=1)
    const = lax.dot_general(
        shift_ref[...], head, dims, precision=HIGH, preferred_element_type=F32
    )
    hb = hb_ref[...]
    hb = jnp.concatenate([hb[:, 0:16], hb[:, 32:48], hb[:, 16:32], hb[:, 48:64]], axis=1)
    const = const + hb
    const_ref[...] = jnp.concatenate([const, const], axis=1)


def prepare(head_weight, mod_scale, mod_shift, head_bias, devs, cin, up, upv, cout):
    count = devs.shape[0]
    hbm = pl.BlockSpec(memory_space=pltpu.HBM)
    vmem = pl.BlockSpec(memory_space=pltpu.VMEM)
    return pl.pallas_call(
        prepare_kernel,
        in_specs=[hbm, vmem, vmem, vmem, vmem, hbm, hbm, vmem, hbm],
        scratch_shapes=[
            pltpu.VMEM(head_weight.shape, F32),
            pltpu.VMEM(cin.shape, BF),
            pltpu.VMEM(up.shape, BF),
            pltpu.VMEM(cout.shape, BF),
            pltpu.SemaphoreType.DMA((4,)),
        ],
        out_shape=[
            jax.ShapeDtypeStruct((count, 128), F32),
            jax.ShapeDtypeStruct((1, 128), F32),
            jax.ShapeDtypeStruct((2, 256, 1536), BF),
            jax.ShapeDtypeStruct((768, 1536), BF),
            jax.ShapeDtypeStruct((2, 384), F32),
            jax.ShapeDtypeStruct((2, 2304, 256), BF),
        ],
        compiler_params=pltpu.CompilerParams(vmem_limit_bytes=20 << 20),
        cost_estimate=pl.CostEstimate(
            flops=20_000_000, bytes_accessed=10_000_000, transcendentals=0
        ),
        name="prepare",
    )(
        in_hbm(head_weight), mod_scale, mod_shift, head_bias, devs, in_hbm(cin), in_hbm(up), upv,
        in_hbm(cout),
    )


def silu_half(half):
    return half + half * jnp.tanh(half)


def decode_kernel(
    group, flags_ref, own_ref, near_ref, core_ref, far_ref, table_ref, const_ref, cin_ref, cinv_ref, up_ref, upv_ref, cout_ref,
    coutv_ref, out_ref, fa, fb, fx, ua, ub, xe, xo, lines, outs, sems,
):
    count = table_ref.shape[0]

    def flagged(row, value):
        return jnp.broadcast_to(flags_ref[row : row + 1, 0 : value.shape[1]], value.shape) > 0.5

    def choose(row, yes, no):
        return jnp.where(flagged(row, yes), yes, no)

    n_stat = 2 * (own_ref.shape[1] - HALF)

    pick_row = lax.broadcasted_iota(jnp.int32, (count + 8, n_stat), 0)
    pick_col = lax.broadcasted_iota(jnp.int32, (count + 8, n_stat), 1)
    of_dev, of_kind = pick_col // STAT, pick_col % STAT
    pick = ((of_kind < 2) & (pick_row == of_dev)) | ((of_kind >= 2) & (pick_row == count))
    pick = pick.astype(F32).astype(BF)
    lane40 = lanes(HALF)
    lane80, sub80 = lanes(TOK_W), lax.broadcasted_iota(jnp.int32, (TOK_W, 128), 0)
    wide = []
    for j in range(3):
        mine, other = [
            jnp.concatenate([a[j, HALF:], b[j, HALF:]], axis=0)
            for a, b in ((own_ref, near_ref), (core_ref, far_ref))
        ]
        wide += [choose(0, mine, other), choose(0, other, mine)]
    wide = jnp.concatenate(wide, axis=1)
    stats = jnp.dot(pick, wide, preferred_element_type=F32)
    means = stats[0:count]
    off = means - jnp.sum(means, axis=0, keepdims=True) * (1.0 / count)
    var = stats[count : count + 1] + group * jnp.sum(off * off, axis=0, keepdims=True)
    inv = lax.rsqrt(var * (1.0 / (count * group)) + EPS)
    off_hi, off_lo = split(off)
    inv_hi, inv_lo = split(inv)
    left = jnp.concatenate(
        [off_hi, off_lo, off_hi, inv_hi, inv_lo, jnp.zeros((14, off.shape[1]), F32)], axis=0
    )
    tab_hi, tab_lo = split(table_ref[...])
    right = jnp.concatenate(
        [
            jnp.concatenate([tab_hi, tab_hi, tab_lo, jnp.zeros((16, 128), F32)], axis=0),
            jnp.concatenate(
                [
                    jnp.zeros((3 * count, 128), F32),
                    jnp.ones((2, 128), F32),
                    jnp.zeros((14, 128), F32),
                ],
                axis=0,
            ),
        ],
        axis=1,
    )
    per_token = jnp.dot(left.T.astype(BF), right.astype(BF), preferred_element_type=F32)
    edge = [[None] * 3 for _ in range(2)]
    first_lanes = jnp.concatenate([lane40, lane40], axis=1) % 128 < 64
    for j in range(3):
        mine, other = [
            a[j, 0:HALF].astype(F32) + b[j, 0:HALF].astype(F32)
            for a, b in ((own_ref, near_ref), (core_ref, far_ref))
        ]
        sums = [choose(0, mine, other), choose(0, other, mine)]
        for f in range(2):
            at = (j * 2 + f) * 128
            token = jnp.where(
                first_lanes, per_token[at : at + HALF], per_token[at + 64 : at + 64 + HALF]
            )
            row = (sums[f] + token[:, 0:128]) * token[:, 128:256] + const_ref[...]
            if j == 0:
                row = choose(1, row, 0.0)
            if j == 2:
                row = choose(2, row, 0.0)
            swapped = pltpu.roll(row, 64, 1)
            both = jnp.concatenate(
                [jnp.where(lane40 < 64, row, swapped), jnp.where(lane40 < 64, swapped, row)],
                axis=0,
            )
            both = pltpu.roll(both, 32, 1)
            before = jnp.where(sub80 == 0, 0.0, pltpu.roll(both, 1, 0))
            after = jnp.where(sub80 == TOK_W - 1, 0.0, pltpu.roll(both, TOK_W - 1, 0))
            edge[f][j] = jnp.where(
                lane80 < 32, before, jnp.where(lane80 >= 96, after, both)
            ).astype(BF)

    def patch(f):
        return jnp.concatenate(
            [jnp.concatenate([edge[f][b], edge[f][b + 1]], axis=1) for b in range(2)], axis=0
        )

    patches = [patch(0), patch(1)]
    both, late = [], []
    for n in range(2):
        cols = slice(n * 768, n * 768 + 768)
        both.append(jnp.dot(jnp.concatenate(patches, axis=0), cin_ref[1, :, cols], preferred_element_type=F32))
        late.append(jnp.dot(patches[0], cin_ref[0, :, cols], preferred_element_type=F32))
    both = jnp.concatenate(both, axis=1)
    pres = [both[0 : 2 * TOK_W], both[2 * TOK_W :] + jnp.concatenate(late, axis=1)]
    bias_in, gain_in = cinv_ref[0:1], cinv_ref[1:2] * 0.5
    sub_one = lax.broadcasted_iota(jnp.int32, (TOK_W, 384), 0)
    zeros_ext = jnp.zeros((TOK_W, 384), F32)
    for f in range(2):
        pre = pres[f]
        for b in range(2):
            for qy in range(2):
                y = 2 * b + qy
                act = []
                for qx in range(2):
                    col = (qy * 2 + qx) * 384
                    v = pre[b * TOK_W : (b + 1) * TOK_W, col : col + 384] + bias_in
                    mean_sq = jnp.sum(v * v, axis=1, keepdims=True) * (1.0 / 384)
                    a = silu_half(v * lax.rsqrt(mean_sq + EPS) * gain_in)
                    if y == 0:
                        a = choose(1, a, 0.0)
                    if y == 3:
                        a = choose(2, a, 0.0)
                    act.append(a)
                even, odd = act
                back = jnp.where(sub_one == 0, 0.0, pltpu.roll(odd, 1, 0))
                even, odd, back = even.astype(BF), odd.astype(BF), back.astype(BF)
                for pair, part in ((y - 1, 1), (y, 0)):
                    if not 0 <= pair < 3:
                        continue
                    at = slice((f * 3 + pair) * TOK_W, (f * 3 + pair + 1) * TOK_W)
                    fa[at, part * 768 : part * 768 + 384] = even
                    fa[at, part * 768 + 384 : part * 768 + 768] = odd
                    fb[at, part * 768 : part * 768 + 384] = back
                    fb[at, part * 768 + 384 : part * 768 + 768] = even
                    fx[f * 3 + pair : f * 3 + pair + 1, part * 768 : part * 768 + 384] = act[1][
                        TOK_W - 1 : TOK_W
                    ]
                    fx[f * 3 + pair : f * 3 + pair + 1, part * 768 + 384 : part * 768 + 768] = (
                        zeros_ext[0:1]
                    )
    del sub_one

    def times_up(x):
        dims = (((1,), (1,)), ((), ()))
        return lax.dot_general(x, up_ref[...], dims, preferred_element_type=F32)

    ua[...] = times_up(fa[...])
    extra_in = jnp.where(
        lax.broadcasted_iota(jnp.int32, (8, 1536), 0) < 6, fx[...], 0.0
    )
    extra_in = jnp.concatenate([extra_in, jnp.zeros((8, 1536), F32)], axis=0).astype(BF)
    fb[6 * TOK_W :] = extra_in
    ub[...] = times_up(fb[...])
    extra = ub[6 * TOK_W : 6 * TOK_W + 8]
    bias_up, gain_up = upv_ref[0:1], upv_ref[1:2] * 0.5

    def second(u):
        v = u + bias_up
        t0, t1, t2 = v[:, 0:128], v[:, 128:256], v[:, 256:384]
        lane = lanes(u.shape[0])
        q = t2 * t2
        left = jnp.sum(t0 * t0 + jnp.where(lane < 64, q, 0.0), axis=1, keepdims=True)
        right = jnp.sum(t1 * t1 + jnp.where(lane < 64, 0.0, q), axis=1, keepdims=True)
        left = lax.rsqrt(left * (1.0 / 192) + EPS)
        right = lax.rsqrt(right * (1.0 / 192) + EPS)
        g = gain_up
        return (
            silu_half(t0 * left * g[:, 0:128]),
            silu_half(t1 * right * g[:, 128:256]),
            silu_half(t2 * jnp.where(lane < 64, left, right) * g[:, 256:384]),
        )

    ends = [second(extra[:, py * 384 : py * 384 + 384]) for py in range(2)]
    for f in range(2):
        for pair in range(3):
            at = (f * 3 + pair) * TOK_W
            for py in range(2):
                y = pair * 2 + py
                cols = slice(py * 384, py * 384 + 384)

                def keep(value, y=y):
                    if y == 0:
                        return choose(1, value, 0.0)
                    if y == 5:
                        return choose(2, value, 0.0)
                    return value

                mid = [keep(t) for t in second(ua[at : at + TOK_W, cols])]
                low = [keep(t) for t in second(ub[at : at + TOK_W, cols])]
                end = [keep(t) for t in ends[py]]
                to = slice(y * TOK_W, (y + 1) * TOK_W)
                first = sub80 == 0
                low[0] = jnp.where(first, 0.0, low[0])
                low[2] = jnp.where(first & (lane80 < 64), 0.0, low[2])
                end[1] = jnp.zeros_like(end[1])
                end[2] = jnp.where(lanes(8) < 64, end[2], 0.0)
                for k in range(3):
                    m = mid[k].astype(BF)
                    xe[f, to, k * 128 : k * 128 + 128] = low[k].astype(BF)
                    xe[f, to, 384 + k * 128 : 512 + k * 128] = m
                    xo[f, to, k * 128 : k * 128 + 128] = m
                    last = end[k][f * 3 + pair : f * 3 + pair + 1]
                    ahead = jnp.where(
                        sub80 == TOK_W - 1, last, pltpu.roll(low[k], TOK_W - 1, 0)
                    )
                    xo[f, to, 384 + k * 128 : 512 + k * 128] = ahead.astype(BF)

    bias_out = coutv_ref[...]
    copies = []
    for f in range(2):
        for side, x in enumerate((xe, xo)):
            acc = None
            for b in range(3):
                rows = slice(b * TOK_W, (b + 4) * TOK_W)
                ks = slice(b * 768, b * 768 + 768)
                term = jnp.dot(x[f, rows], cout_ref[1, ks], preferred_element_type=F32)
                acc = term if acc is None else acc + term
                if f == 1:
                    acc = acc + jnp.dot(x[0, rows], cout_ref[0, ks], preferred_element_type=F32)
            for j in range(4):
                for o in range(2):
                    lines[f, j, pl.ds(2 * side + o, TOK_W, stride=4), :] = (
                        acc[j * TOK_W : (j + 1) * TOK_W, o * 128 : o * 128 + 128] + bias_out
                    )
        for j in range(4):
            outs[f, j] = lines[f, j].T[0:96].astype(BF)
        copy = pltpu.make_async_copy(outs.at[f], out_ref.at[f], sems.at[f])
        copy.start()
        copies.append(copy)
    for copy in copies:
        copy.wait()


def decode(group, flags, pieces, table, const, cin, cinv, up, upv, cout, coutv):
    vmem = pl.BlockSpec(memory_space=pltpu.VMEM)
    return pl.pallas_call(
        functools.partial(decode_kernel, float(group)),
        in_specs=[vmem] * 13,
        out_specs=pl.BlockSpec(memory_space=pltpu.HBM),
        out_shape=jax.ShapeDtypeStruct((2, 4, 96, 4 * TOK_W), BF),
        scratch_shapes=[
            pltpu.VMEM((6 * TOK_W, 1536), BF),
            pltpu.VMEM((6 * TOK_W + 16, 1536), BF),
            pltpu.VMEM((8, 1536), F32),
            pltpu.VMEM((6 * TOK_W, 768), F32),
            pltpu.VMEM((6 * TOK_W + 16, 768), F32),
            pltpu.VMEM((2, 6 * TOK_W, 768), BF),
            pltpu.VMEM((2, 6 * TOK_W, 768), BF),
            pltpu.VMEM((2, 4, 4 * TOK_W, 128), F32),
            pltpu.VMEM((2, 4, 96, 4 * TOK_W), BF),
            pltpu.SemaphoreType.DMA((2,)),
        ],
        compiler_params=pltpu.CompilerParams(vmem_limit_bytes=24 << 20),
        cost_estimate=pl.CostEstimate(
            flops=5_000_000_000, bytes_accessed=8_000_000, transcendentals=1_300_000
        ),
        name="decode",
    )(flags, *pieces, table, const, cin, cinv, up, upv, cout, coutv)


def exchange(block, mask, count):
    return lax.ppermute(block, "seq", [(i, i ^ mask) for i in range(count)])


def merged(own, received):
    total = own[:, :HALF].astype(F32)
    for item in received:
        total = total + item[:, :HALF].astype(F32)
    return jnp.concatenate(
        [total.astype(BF), own[:, HALF:]] + [item[:, HALF:] for item in received], axis=1
    )


def cut(block, start, size):
    return lax.dynamic_slice_in_dim(block, start, size, 0)


def steps_of(count):
    bit = count.bit_length() - 3
    steps = [[2 << bit, 1 << bit, 3 << bit]]
    while bit > 2:
        bit -= 1
        steps.append([1 << bit])
    return steps


def device_order(count):
    order = [0]
    for masks in steps_of(count):
        order = order + [o ^ mask for mask in masks for o in order]
    order = order + [o ^ 2 for o in order]
    return np.asarray([o + c for o in order for c in range(2)], np.int32)


def gather_rows(own, give, weights, ready, me, count):
    block = (own.astype(F32) + exchange(give, 1, count).astype(F32)).astype(BF)
    block, weights = lax.optimization_barrier((block, weights))

    def window(base, size):
        return jnp.clip(base - 1, 0, count - size)

    start = jnp.int32(0)
    for masks in steps_of(count):
        unit = min(masks)
        size = unit + 2
        base = (me // unit) * unit
        new = window(base, size)
        received = [
            exchange(cut(block, window(base ^ mask, size) - start, size), mask, count)
            for mask in masks
        ]
        block = merged(cut(block, new - start, size), received)
        if len(masks) > 1:
            block, weights = lax.optimization_barrier((block, ready(weights)))
        start = new
    padded = jnp.pad(block, ((1, 1), (0, 0), (0, 0)))
    pieces = [cut(padded, me - start, 3)]
    for mask in (2, 1, 3):
        pieces.append(exchange(cut(padded, (me ^ mask) - start, 3), mask, count))
    return pieces, weights


def local(
    hidden,
    mod_shift,
    mod_scale,
    head_weight,
    head_bias,
    conv_in_weight,
    conv_in_bias,
    gain_in,
    up_weight,
    up_bias,
    gain_up,
    out_weight,
    out_bias,
):
    count = lax.axis_size("seq")
    me = lax.axis_index("seq")
    feats = hidden.shape[1]
    flags = jnp.stack([me % 2 == 0, me > 0, me < count - 1]).astype(F32)
    flags = jnp.broadcast_to(flags[:, None], (3, 384))
    own, give = project(hidden, head_weight, mod_scale[None])
    weights = (head_weight, conv_in_weight, jnp.swapaxes(up_weight, 2, 3), out_weight)

    def ready(parts):
        head_again, cin, up, cout = parts
        return prepare(
            head_again, mod_scale[None], mod_shift[None], head_bias[None],
            (((me // 2) * 2) ^ device_order(count))[:, None],
            cin, up, jnp.stack([up_bias, gain_up]), cout,
        )

    pieces, weights = gather_rows(own, give, weights, ready, me, count)
    table, const, cin, up, upv, cout = weights
    cinv = jnp.stack([conv_in_bias, gain_in])
    coutv = jnp.pad(out_bias, (0, 32))[None]
    out = decode(feats, flags, pieces, table, const, cin, cinv, up, upv, cout, coutv)
    return jnp.swapaxes(out, 2, 3)


def solution(mesh):
    placed = (P("grp", "seq", None), P(), P(), P(), P(), P(), P(), P(), P(), P(), P(), P(), P())
    return jax.shard_map(
        local, mesh=mesh, in_specs=placed, out_specs=P("grp", "seq", None, None), check_vma=False
    )
```

```python
import functools
import jax
import jax.numpy as jnp
import numpy as np
from jax import lax
from jax.experimental import pallas as pl
from jax.experimental.pallas import tpu as pltpu
from jax.sharding import PartitionSpec as P

TOK_W = 80
HALF = TOK_W // 2
STAT = 4
EPS = 1e-06
HIGH = lax.Precision.HIGHEST
BF = jnp.bfloat16
F32 = jnp.float32


def in_hbm(value):
    return pltpu.with_memory_space_constraint(value, pltpu.HBM)


def split(values):
    high = values.astype(BF).astype(F32)
    return high, values - high


def lanes(rows):
    return lax.broadcasted_iota(jnp.int32, (rows, 128), 1)


def frame_sums(x, stack, gain_sum, core, out_ref):
    feats, tokens = x.shape
    width = 640
    lane40 = lanes(HALF)
    lane = lanes(8)
    sub = lax.broadcasted_iota(jnp.int32, (8, 128), 0)
    for i in range(tokens // width):
        block = x[:, i * width : (i + 1) * width]
        prod = jnp.dot(stack, block, preferred_element_type=F32)
        mean = prod[128:129] * (1.0 / feats)
        part = prod[0:64] + prod[64:128] - gain_sum * mean
        off = block.astype(F32) - mean
        second = jnp.sum(off * off, axis=0, keepdims=True)
        m_hi, m_lo = split(mean)
        s_hi, s_lo = split(second)
        stats = jnp.concatenate([m_hi, m_lo, s_hi, s_lo] * 2, axis=0)
        flat = jnp.concatenate([part, part], axis=0).T
        for row in range(width // TOK_W):
            first = row * TOK_W
            sums = jnp.where(
                lane40 < 64, flat[first : first + HALF], flat[first + HALF : first + TOK_W]
            )
            picks = []
            for h in range(2):
                at = first + h * HALF
                base = (at // 128) * 128
                span = min(256, width - base)
                window = stats[:, base : base + span]
                shift = (64 * h - (at - base)) % span
                if shift:
                    window = pltpu.roll(window, shift, 1)
                picks.append(window[:, :128])
            tail = jnp.where(
                lane < HALF,
                picks[0],
                jnp.where((lane >= 64) & (lane < 64 + HALF), picks[1], 0.0),
            )
            tail = jnp.where(lax.div(sub, STAT) == core, tail, 0.0)
            out_ref[i * (width // TOK_W) + row] = jnp.concatenate([sums, tail], axis=0).astype(BF)


def project_give_kernel(
    hid_ref, w_ref, scale_ref, give_ref, own_ref, stack_ref, gsum_ref,
    hid, w, scale, sems,
):
    feats = hid_ref.shape[1]
    me = lax.axis_index("seq")
    core = me & 1
    wide = w.shape[1]
    at = jnp.minimum(lax.div(me * feats, 128) * 128, w_ref.shape[1] - wide)
    at = pl.multiple_of(at, 128)
    copies = [
        pltpu.make_async_copy(w_ref.at[:, pl.ds(at, wide)], w, sems.at[0]),
        pltpu.make_async_copy(scale_ref.at[:, pl.ds(at, wide)], scale, sems.at[1]),
        pltpu.make_async_copy(hid_ref.at[1 - core], hid, sems.at[2]),
        pltpu.make_async_copy(hid_ref.at[core], own_ref, sems.at[3]),
    ]
    for copy in copies:
        copy.start()
    copies[0].wait()
    copies[1].wait()
    gain = w[...] * (1.0 + scale[...])
    gain = pltpu.roll(gain, wide - (me * feats - at), 1)[:, :feats]
    gain = jnp.concatenate([gain[0:16], gain[32:48], gain[16:32], gain[48:64]], axis=0)
    high, low = split(gain)
    gain_sum = jnp.sum(gain, axis=1, keepdims=True)
    stack = jnp.concatenate([high, low, jnp.ones((16, feats), F32)], axis=0).astype(BF)
    stack_ref[...] = stack
    gsum_ref[...] = jnp.broadcast_to(gain_sum, gsum_ref.shape)
    copies[2].wait()
    frame_sums(hid[...], stack, gain_sum, core, give_ref)
    copies[3].wait()


def project_own_kernel(hid_ref, stack_ref, gsum_ref, own_ref):
    frame_sums(
        hid_ref[...], stack_ref[...], gsum_ref[:, 0:1], lax.axis_index("seq") & 1, own_ref
    )


def project(hidden, head_weight, scale):
    _, feats, tokens = hidden.shape
    rows = tokens // TOK_W
    wide = min(head_weight.shape[1], (feats + 127) // 128 * 128 + 128)
    hbm = pl.BlockSpec(memory_space=pltpu.HBM)
    vmem = pl.BlockSpec(memory_space=pltpu.VMEM)
    sums = jax.ShapeDtypeStruct((rows, HALF + 2 * STAT, 128), BF)
    params = pltpu.CompilerParams(vmem_limit_bytes=16 << 20)
    give, frame, stack, gsum = pl.pallas_call(
        project_give_kernel,
        in_specs=[hbm, hbm, hbm],
        out_specs=[vmem] * 4,
        out_shape=[
            sums,
            jax.ShapeDtypeStruct((feats, tokens), BF),
            jax.ShapeDtypeStruct((144, feats), BF),
            jax.ShapeDtypeStruct((64, 128), F32),
        ],
        scratch_shapes=[
            pltpu.VMEM((feats, tokens), BF),
            pltpu.VMEM((64, wide), F32),
            pltpu.VMEM((1, wide), F32),
            pltpu.SemaphoreType.DMA((4,)),
        ],
        compiler_params=params,
        name="project_give",
    )(in_hbm(hidden), in_hbm(head_weight), in_hbm(scale))

    own = pl.pallas_call(
        project_own_kernel,
        in_specs=[vmem, vmem, vmem],
        out_specs=vmem,
        out_shape=sums,
        compiler_params=params,
        cost_estimate=pl.CostEstimate(
            flops=2 * 144 * feats * tokens, bytes_accessed=1_300_000, transcendentals=0
        ),
        name="project_own",
    )(frame, stack, gsum)
    return own, give


def prepare_first(cin_ref, cin_out):
    zero16 = jnp.zeros((16, 384), BF)
    for tap in range(2):
        for ly in range(4):
            for lx in range(4):
                row = (ly // 2) * 128 + lx * 32 + (ly % 2) * 16
                for qy in range(2):
                    for qx in range(2):
                        dy, dx = ly - qy, lx - qx
                        good = 0 <= dy < 3 and 0 <= dx < 3
                        piece = cin_ref[tap + 1, dy, dx] if good else zero16
                        col = (qy * 2 + qx) * 384
                        cin_out[tap, row : row + 16, col : col + 384] = piece


def prepare_up(up_ref, up_out):
    taps = {(0, 0): (0, 1), (0, 1): (2,), (1, 0): (0,), (1, 1): (1, 2)}
    for dx in range(2):
        for dy in range(2):
            for py in range(2):
                for px in range(2):
                    total = None
                    for b in taps[py, dy]:
                        for e in taps[px, dx]:
                            term = up_ref[b, e].astype(F32)
                            total = term if total is None else total + term
                    total = total.astype(BF)
                    k = slice((dy * 2 + dx) * 384, (dy * 2 + dx + 1) * 384)
                    n = py * 384
                    up_out[n + px * 128 : n + px * 128 + 128, k] = total[0:128]
                    up_out[n + 256 + px * 64 : n + 320 + px * 64, k] = total[128:192]


def prepare_last(cout_ref, cout_out):
    cout_out[...] = jnp.zeros(cout_out.shape, BF)
    for tap in range(2):
        for b in range(3):
            for v in range(2):
                for s in range(2):
                    for o in range(2):
                        e = 2 * v + s - o
                        if not 0 <= e < 3:
                            continue
                        row = b * 768 + v * 384
                        weight = cout_ref[tap + 1, b, e]
                        lo = row + s * 128
                        hi = row + 256 + s * 64
                        cout_out[tap, lo : lo + 128, o * 128 : o * 128 + 96] = weight[0:128]
                        cout_out[tap, hi : hi + 64, o * 128 : o * 128 + 96] = weight[128:192]


def prepare_kernel(
    w_ref, scale_ref, shift_ref, hb_ref, dev_ref, cin_ref, up_ref, upv_ref, cout_ref,
    table_ref, const_ref, cin_out, up_out, upv_out, cout_out, w, cin, up, cout, sems,
):
    copies = [
        pltpu.make_async_copy(source, target, sems.at[i])
        for i, (source, target) in enumerate(
            ((cin_ref, cin), (up_ref, up), (cout_ref, cout), (w_ref, w))
        )
    ]
    for copy in copies:
        copy.start()
    copies[0].wait()
    prepare_first(cin, cin_out)
    copies[1].wait()
    prepare_up(up, up_out)
    vec = upv_ref[...]
    upv_out[...] = jnp.concatenate(
        [vec[:, 0:128], vec[:, 0:128], vec[:, 128:192], vec[:, 128:192]], axis=1
    )
    copies[2].wait()
    prepare_last(cout, cout_out)
    copies[3].wait()
    feats = w_ref.shape[1] // dev_ref.shape[0]
    head = w[...]
    head = jnp.concatenate([head[0:16], head[32:48], head[16:32], head[48:64]], axis=0)
    gain = head * (1.0 + scale_ref[...])
    count = dev_ref.shape[0]
    place = lax.broadcasted_iota(jnp.int32, (count, w_ref.shape[1]), 1) - dev_ref[...] * feats
    inside = ((place >= 0) & (place < feats)).astype(F32)
    dims = (((1,), (1,)), ((), ()))
    sums = lax.dot_general(inside, gain, dims, precision=HIGH, preferred_element_type=F32)
    table_ref[...] = jnp.concatenate([sums, sums], axis=1)
    const = lax.dot_general(
        shift_ref[...], head, dims, precision=HIGH, preferred_element_type=F32
    )
    hb = hb_ref[...]
    hb = jnp.concatenate([hb[:, 0:16], hb[:, 32:48], hb[:, 16:32], hb[:, 48:64]], axis=1)
    const = const + hb
    const_ref[...] = jnp.concatenate([const, const], axis=1)


def prepare(head_weight, mod_scale, mod_shift, head_bias, devs, cin, up, upv, cout):
    count = devs.shape[0]
    hbm = pl.BlockSpec(memory_space=pltpu.HBM)
    vmem = pl.BlockSpec(memory_space=pltpu.VMEM)
    return pl.pallas_call(
        prepare_kernel,
        in_specs=[hbm, vmem, vmem, vmem, vmem, hbm, hbm, vmem, hbm],
        scratch_shapes=[
            pltpu.VMEM(head_weight.shape, F32),
            pltpu.VMEM(cin.shape, BF),
            pltpu.VMEM(up.shape, BF),
            pltpu.VMEM(cout.shape, BF),
            pltpu.SemaphoreType.DMA((4,)),
        ],
        out_shape=[
            jax.ShapeDtypeStruct((count, 128), F32),
            jax.ShapeDtypeStruct((1, 128), F32),
            jax.ShapeDtypeStruct((2, 256, 1536), BF),
            jax.ShapeDtypeStruct((768, 1536), BF),
            jax.ShapeDtypeStruct((2, 384), F32),
            jax.ShapeDtypeStruct((2, 2304, 256), BF),
        ],
        compiler_params=pltpu.CompilerParams(vmem_limit_bytes=20 << 20),
        cost_estimate=pl.CostEstimate(
            flops=20_000_000, bytes_accessed=10_000_000, transcendentals=0
        ),
        name="prepare",
    )(
        in_hbm(head_weight), mod_scale, mod_shift, head_bias, devs, in_hbm(cin), in_hbm(up), upv,
        in_hbm(cout),
    )


def silu_half(half):
    return half + half * jnp.tanh(half)


def decode_kernel(
    group, flags_ref, own_ref, near_ref, core_ref, far_ref, table_ref, const_ref, cin_ref, cinv_ref, up_ref, upv_ref, cout_ref,
    coutv_ref, out_ref, fa, fb, fx, ua, ub, xe, xo, lines, outs, sems,
):
    count = table_ref.shape[0]

    def flagged(row, value):
        return jnp.broadcast_to(flags_ref[row : row + 1, 0 : value.shape[1]], value.shape) > 0.5

    def choose(row, yes, no):
        return jnp.where(flagged(row, yes), yes, no)

    n_stat = 2 * (own_ref.shape[1] - HALF)

    pick_row = lax.broadcasted_iota(jnp.int32, (count + 8, n_stat), 0)
    pick_col = lax.broadcasted_iota(jnp.int32, (count + 8, n_stat), 1)
    of_dev, of_kind = pick_col // STAT, pick_col % STAT
    pick = ((of_kind < 2) & (pick_row == of_dev)) | ((of_kind >= 2) & (pick_row == count))
    pick = pick.astype(F32).astype(BF)
    lane40 = lanes(HALF)
    lane80, sub80 = lanes(TOK_W), lax.broadcasted_iota(jnp.int32, (TOK_W, 128), 0)
    wide = []
    for j in range(3):
        mine, other = [
            jnp.concatenate([a[j, HALF:], b[j, HALF:]], axis=0)
            for a, b in ((own_ref, near_ref), (core_ref, far_ref))
        ]
        wide += [choose(0, mine, other), choose(0, other, mine)]
    wide = jnp.concatenate(wide, axis=1)
    stats = jnp.dot(pick, wide, preferred_element_type=F32)
    means = stats[0:count]
    off = means - jnp.sum(means, axis=0, keepdims=True) * (1.0 / count)
    var = stats[count : count + 1] + group * jnp.sum(off * off, axis=0, keepdims=True)
    inv = lax.rsqrt(var * (1.0 / (count * group)) + EPS)
    off_hi, off_lo = split(off)
    inv_hi, inv_lo = split(inv)
    left = jnp.concatenate(
        [off_hi, off_lo, off_hi, inv_hi, inv_lo, jnp.zeros((14, off.shape[1]), F32)], axis=0
    )
    tab_hi, tab_lo = split(table_ref[...])
    right = jnp.concatenate(
        [
            jnp.concatenate([tab_hi, tab_hi, tab_lo, jnp.zeros((16, 128), F32)], axis=0),
            jnp.concatenate(
                [
                    jnp.zeros((3 * count, 128), F32),
                    jnp.ones((2, 128), F32),
                    jnp.zeros((14, 128), F32),
                ],
                axis=0,
            ),
        ],
        axis=1,
    )
    per_token = jnp.dot(left.T.astype(BF), right.astype(BF), preferred_element_type=F32)
    edge = [[None] * 3 for _ in range(2)]
    first_lanes = jnp.concatenate([lane40, lane40], axis=1) % 128 < 64
    for j in range(3):
        mine, other = [
            a[j, 0:HALF].astype(F32) + b[j, 0:HALF].astype(F32)
            for a, b in ((own_ref, near_ref), (core_ref, far_ref))
        ]
        sums = [choose(0, mine, other), choose(0, other, mine)]
        for f in range(2):
            at = (j * 2 + f) * 128
            token = jnp.where(
                first_lanes, per_token[at : at + HALF], per_token[at + 64 : at + 64 + HALF]
            )
            row = (sums[f] + token[:, 0:128]) * token[:, 128:256] + const_ref[...]
            if j == 0:
                row = choose(1, row, 0.0)
            if j == 2:
                row = choose(2, row, 0.0)
            swapped = pltpu.roll(row, 64, 1)
            both = jnp.concatenate(
                [jnp.where(lane40 < 64, row, swapped), jnp.where(lane40 < 64, swapped, row)],
                axis=0,
            )
            both = pltpu.roll(both, 32, 1)
            before = jnp.where(sub80 == 0, 0.0, pltpu.roll(both, 1, 0))
            after = jnp.where(sub80 == TOK_W - 1, 0.0, pltpu.roll(both, TOK_W - 1, 0))
            edge[f][j] = jnp.where(
                lane80 < 32, before, jnp.where(lane80 >= 96, after, both)
            ).astype(BF)

    def patch(f):
        return jnp.concatenate(
            [jnp.concatenate([edge[f][b], edge[f][b + 1]], axis=1) for b in range(2)], axis=0
        )

    patches = [patch(0), patch(1)]
    both, late = [], []
    for n in range(2):
        cols = slice(n * 768, n * 768 + 768)
        both.append(jnp.dot(jnp.concatenate(patches, axis=0), cin_ref[1, :, cols], preferred_element_type=F32))
        late.append(jnp.dot(patches[0], cin_ref[0, :, cols], preferred_element_type=F32))
    both = jnp.concatenate(both, axis=1)
    pres = [both[0 : 2 * TOK_W], both[2 * TOK_W :] + jnp.concatenate(late, axis=1)]
    bias_in, gain_in = cinv_ref[0:1], cinv_ref[1:2] * 0.5
    sub_one = lax.broadcasted_iota(jnp.int32, (TOK_W, 384), 0)
    zeros_ext = jnp.zeros((TOK_W, 384), F32)
    for f in range(2):
        pre = pres[f]
        for b in range(2):
            for qy in range(2):
                y = 2 * b + qy
                act = []
                for qx in range(2):
                    col = (qy * 2 + qx) * 384
                    v = pre[b * TOK_W : (b + 1) * TOK_W, col : col + 384] + bias_in
                    mean_sq = jnp.sum(v * v, axis=1, keepdims=True) * (1.0 / 384)
                    a = silu_half(v * lax.rsqrt(mean_sq + EPS) * gain_in)
                    if y == 0:
                        a = choose(1, a, 0.0)
                    if y == 3:
                        a = choose(2, a, 0.0)
                    act.append(a)
                even, odd = act
                back = jnp.where(sub_one == 0, 0.0, pltpu.roll(odd, 1, 0))
                even, odd, back = even.astype(BF), odd.astype(BF), back.astype(BF)
                for pair, part in ((y - 1, 1), (y, 0)):
                    if not 0 <= pair < 3:
                        continue
                    at = slice((f * 3 + pair) * TOK_W, (f * 3 + pair + 1) * TOK_W)
                    fa[at, part * 768 : part * 768 + 384] = even
                    fa[at, part * 768 + 384 : part * 768 + 768] = odd
                    fb[at, part * 768 : part * 768 + 384] = back
                    fb[at, part * 768 + 384 : part * 768 + 768] = even
                    fx[f * 3 + pair : f * 3 + pair + 1, part * 768 : part * 768 + 384] = act[1][
                        TOK_W - 1 : TOK_W
                    ]
                    fx[f * 3 + pair : f * 3 + pair + 1, part * 768 + 384 : part * 768 + 768] = (
                        zeros_ext[0:1]
                    )
    del sub_one

    extra_in = jnp.where(
        lax.broadcasted_iota(jnp.int32, (8, 1536), 0) < 6, fx[...], 0.0
    )
    extra_in = jnp.concatenate([extra_in, jnp.zeros((8, 1536), F32)], axis=0).astype(BF)
    fb[6 * TOK_W :] = extra_in
    chunk = 3 * TOK_W
    for n in range(0, 768, 256):
        for first in (0, chunk):
            for given, result in ((fa, ua), (fb, ub)):
                rows = slice(first, first + chunk if first == 0 else given.shape[0])
                result[rows, n : n + 256] = lax.dot_general(
                    given[rows], up_ref[n : n + 256], (((1,), (1,)), ((), ())),
                    preferred_element_type=F32,
                )
    extra = ub[6 * TOK_W : 6 * TOK_W + 8]
    bias_up, gain_up = upv_ref[0:1], upv_ref[1:2] * 0.5

    def second(u):
        v = u + bias_up
        t0, t1, t2 = v[:, 0:128], v[:, 128:256], v[:, 256:384]
        lane = lanes(u.shape[0])
        q = t2 * t2
        left = jnp.sum(t0 * t0 + jnp.where(lane < 64, q, 0.0), axis=1, keepdims=True)
        right = jnp.sum(t1 * t1 + jnp.where(lane < 64, 0.0, q), axis=1, keepdims=True)
        left = lax.rsqrt(left * (1.0 / 192) + EPS)
        right = lax.rsqrt(right * (1.0 / 192) + EPS)
        g = gain_up
        return (
            silu_half(t0 * left * g[:, 0:128]),
            silu_half(t1 * right * g[:, 128:256]),
            silu_half(t2 * jnp.where(lane < 64, left, right) * g[:, 256:384]),
        )

    ends = [second(extra[:, py * 384 : py * 384 + 384]) for py in range(2)]
    for f in range(2):
        for pair in range(3):
            at = (f * 3 + pair) * TOK_W
            for py in range(2):
                y = pair * 2 + py
                cols = slice(py * 384, py * 384 + 384)

                def keep(value, y=y):
                    if y == 0:
                        return choose(1, value, 0.0)
                    if y == 5:
                        return choose(2, value, 0.0)
                    return value

                mid = [keep(t) for t in second(ua[at : at + TOK_W, cols])]
                low = [keep(t) for t in second(ub[at : at + TOK_W, cols])]
                end = [keep(t) for t in ends[py]]
                to = slice(y * TOK_W, (y + 1) * TOK_W)
                first = sub80 == 0
                low[0] = jnp.where(first, 0.0, low[0])
                low[2] = jnp.where(first & (lane80 < 64), 0.0, low[2])
                end[1] = jnp.zeros_like(end[1])
                end[2] = jnp.where(lanes(8) < 64, end[2], 0.0)
                for k in range(3):
                    m = mid[k].astype(BF)
                    xe[f, to, k * 128 : k * 128 + 128] = low[k].astype(BF)
                    xe[f, to, 384 + k * 128 : 512 + k * 128] = m
                    xo[f, to, k * 128 : k * 128 + 128] = m
                    last = end[k][f * 3 + pair : f * 3 + pair + 1]
                    ahead = jnp.where(
                        sub80 == TOK_W - 1, last, pltpu.roll(low[k], TOK_W - 1, 0)
                    )
                    xo[f, to, 384 + k * 128 : 512 + k * 128] = ahead.astype(BF)

    bias_out = coutv_ref[...]
    copies = []
    for f in range(2):
        for side, x in enumerate((xe, xo)):
            acc = None
            for b in range(3):
                rows = slice(b * TOK_W, (b + 4) * TOK_W)
                ks = slice(b * 768, b * 768 + 768)
                term = jnp.dot(x[f, rows], cout_ref[1, ks], preferred_element_type=F32)
                acc = term if acc is None else acc + term
                if f == 1:
                    acc = acc + jnp.dot(x[0, rows], cout_ref[0, ks], preferred_element_type=F32)
            for j in range(4):
                for o in range(2):
                    lines[f, j, pl.ds(2 * side + o, TOK_W, stride=4), :] = (
                        acc[j * TOK_W : (j + 1) * TOK_W, o * 128 : o * 128 + 128] + bias_out
                    )
        for j in range(4):
            outs[f, j] = lines[f, j].T[0:96].astype(BF)
        copy = pltpu.make_async_copy(outs.at[f], out_ref.at[f], sems.at[f])
        copy.start()
        copies.append(copy)
    for copy in copies:
        copy.wait()


def decode(group, flags, pieces, table, const, cin, cinv, up, upv, cout, coutv):
    vmem = pl.BlockSpec(memory_space=pltpu.VMEM)
    return pl.pallas_call(
        functools.partial(decode_kernel, float(group)),
        in_specs=[vmem] * 13,
        out_specs=pl.BlockSpec(memory_space=pltpu.HBM),
        out_shape=jax.ShapeDtypeStruct((2, 4, 96, 4 * TOK_W), BF),
        scratch_shapes=[
            pltpu.VMEM((6 * TOK_W, 1536), BF),
            pltpu.VMEM((6 * TOK_W + 16, 1536), BF),
            pltpu.VMEM((8, 1536), F32),
            pltpu.VMEM((6 * TOK_W, 768), F32),
            pltpu.VMEM((6 * TOK_W + 16, 768), F32),
            pltpu.VMEM((2, 6 * TOK_W, 768), BF),
            pltpu.VMEM((2, 6 * TOK_W, 768), BF),
            pltpu.VMEM((2, 4, 4 * TOK_W, 128), F32),
            pltpu.VMEM((2, 4, 96, 4 * TOK_W), BF),
            pltpu.SemaphoreType.DMA((2,)),
        ],
        compiler_params=pltpu.CompilerParams(vmem_limit_bytes=24 << 20),
        cost_estimate=pl.CostEstimate(
            flops=5_000_000_000, bytes_accessed=8_000_000, transcendentals=1_300_000
        ),
        name="decode",
    )(flags, *pieces, table, const, cin, cinv, up, upv, cout, coutv)


def exchange(block, mask, count):
    return lax.ppermute(block, "seq", [(i, i ^ mask) for i in range(count)])


def merged(own, received):
    total = own[:, :HALF].astype(F32)
    for item in received:
        total = total + item[:, :HALF].astype(F32)
    return jnp.concatenate(
        [total.astype(BF), own[:, HALF:]] + [item[:, HALF:] for item in received], axis=1
    )


def cut(block, start, size):
    return lax.dynamic_slice_in_dim(block, start, size, 0)


def steps_of(count):
    bit = count.bit_length() - 3
    steps = [[2 << bit, 1 << bit, 3 << bit]]
    while bit > 2:
        bit -= 1
        steps.append([1 << bit])
    return steps


def device_order(count):
    order = [0]
    for masks in steps_of(count):
        order = order + [o ^ mask for mask in masks for o in order]
    order = order + [o ^ 2 for o in order]
    return np.asarray([o + c for o in order for c in range(2)], np.int32)


def gather_rows(own, give, weights, ready, me, count):
    block = (own.astype(F32) + exchange(give, 1, count).astype(F32)).astype(BF)
    block, weights = lax.optimization_barrier((block, weights))

    def window(base, size):
        return jnp.clip(base - 1, 0, count - size)

    start = jnp.int32(0)
    for masks in steps_of(count):
        unit = min(masks)
        size = unit + 2
        base = (me // unit) * unit
        new = window(base, size)
        received = [
            exchange(cut(block, window(base ^ mask, size) - start, size), mask, count)
            for mask in masks
        ]
        block = merged(cut(block, new - start, size), received)
        if len(masks) > 1:
            block, weights = lax.optimization_barrier((block, ready(weights)))
        start = new
    padded = jnp.pad(block, ((1, 1), (0, 0), (0, 0)))
    pieces = [cut(padded, me - start, 3)]
    for mask in (2, 1, 3):
        pieces.append(exchange(cut(padded, (me ^ mask) - start, 3), mask, count))
    return pieces, weights


def local(
    hidden,
    mod_shift,
    mod_scale,
    head_weight,
    head_bias,
    conv_in_weight,
    conv_in_bias,
    gain_in,
    up_weight,
    up_bias,
    gain_up,
    out_weight,
    out_bias,
):
    count = lax.axis_size("seq")
    me = lax.axis_index("seq")
    feats = hidden.shape[1]
    flags = jnp.stack([me % 2 == 0, me > 0, me < count - 1]).astype(F32)
    flags = jnp.broadcast_to(flags[:, None], (3, 384))
    own, give = project(hidden, head_weight, mod_scale[None])
    weights = (head_weight, conv_in_weight, jnp.swapaxes(up_weight, 2, 3), out_weight)

    def ready(parts):
        head_again, cin, up, cout = parts
        return flags, prepare(
            head_again, mod_scale[None], mod_shift[None], head_bias[None],
            (((me // 2) * 2) ^ device_order(count))[:, None],
            cin, up, jnp.stack([up_bias, gain_up]), cout,
        )

    pieces, weights = gather_rows(own, give, weights, ready, me, count)
    flags, (table, const, cin, up, upv, cout) = weights
    cinv = jnp.stack([conv_in_bias, gain_in])
    coutv = jnp.pad(out_bias, (0, 32))[None]
    out = decode(feats, flags, pieces, table, const, cin, cinv, up, upv, cout, coutv)
    return jnp.swapaxes(out, 2, 3)


def solution(mesh):
    placed = (P("grp", "seq", None), P(), P(), P(), P(), P(), P(), P(), P(), P(), P(), P(), P())
    return jax.shard_map(
        local, mesh=mesh, in_specs=placed, out_specs=P("grp", "seq", None, None), check_vma=False
    )
```

```python
import functools
import jax
import jax.numpy as jnp
import numpy as np
from jax import lax
from jax.experimental import pallas as pl
from jax.experimental.pallas import tpu as pltpu
from jax.sharding import PartitionSpec as P

TOK_W = 80
HALF = TOK_W // 2
STAT = 4
EPS = 1e-06
HIGH = lax.Precision.HIGHEST
BF = jnp.bfloat16
F32 = jnp.float32


def in_hbm(value):
    return pltpu.with_memory_space_constraint(value, pltpu.HBM)


def split(values):
    high = values.astype(BF).astype(F32)
    return high, values - high


def lanes(rows):
    return lax.broadcasted_iota(jnp.int32, (rows, 128), 1)


def frame_sums(x, stack, gain_sum, core, out_ref):
    feats, tokens = x.shape
    width = 640
    lane40 = lanes(HALF)
    lane = lanes(8)
    sub = lax.broadcasted_iota(jnp.int32, (8, 128), 0)
    for i in range(tokens // width):
        block = x[:, i * width : (i + 1) * width]
        prod = jnp.dot(stack, block, preferred_element_type=F32)
        mean = prod[128:129] * (1.0 / feats)
        part = prod[0:64] + prod[64:128] - gain_sum * mean
        off = block.astype(F32) - mean
        second = jnp.sum(off * off, axis=0, keepdims=True)
        m_hi, m_lo = split(mean)
        s_hi, s_lo = split(second)
        stats = jnp.concatenate([m_hi, m_lo, s_hi, s_lo] * 2, axis=0)
        flat = jnp.concatenate([part, part], axis=0).T
        for row in range(width // TOK_W):
            first = row * TOK_W
            sums = jnp.where(
                lane40 < 64, flat[first : first + HALF], flat[first + HALF : first + TOK_W]
            )
            picks = []
            for h in range(2):
                at = first + h * HALF
                base = (at // 128) * 128
                span = min(256, width - base)
                window = stats[:, base : base + span]
                shift = (64 * h - (at - base)) % span
                if shift:
                    window = pltpu.roll(window, shift, 1)
                picks.append(window[:, :128])
            tail = jnp.where(
                lane < HALF,
                picks[0],
                jnp.where((lane >= 64) & (lane < 64 + HALF), picks[1], 0.0),
            )
            tail = jnp.where(lax.div(sub, STAT) == core, tail, 0.0)
            out_ref[i * (width // TOK_W) + row] = jnp.concatenate([sums, tail], axis=0).astype(BF)


def project_give_kernel(
    hid_ref, w_ref, scale_ref, give_ref, own_ref, stack_ref, gsum_ref,
    hid, w, scale, sems,
):
    feats = hid_ref.shape[1]
    me = lax.axis_index("seq")
    core = me & 1
    wide = w.shape[1]
    at = jnp.minimum(lax.div(me * feats, 128) * 128, w_ref.shape[1] - wide)
    at = pl.multiple_of(at, 128)
    copies = [
        pltpu.make_async_copy(w_ref.at[:, pl.ds(at, wide)], w, sems.at[0]),
        pltpu.make_async_copy(scale_ref.at[:, pl.ds(at, wide)], scale, sems.at[1]),
        pltpu.make_async_copy(hid_ref.at[1 - core], hid, sems.at[2]),
        pltpu.make_async_copy(hid_ref.at[core], own_ref, sems.at[3]),
    ]
    for copy in copies:
        copy.start()
    copies[0].wait()
    copies[1].wait()
    gain = w[...] * (1.0 + scale[...])
    gain = pltpu.roll(gain, wide - (me * feats - at), 1)[:, :feats]
    gain = jnp.concatenate([gain[0:16], gain[32:48], gain[16:32], gain[48:64]], axis=0)
    high, low = split(gain)
    gain_sum = jnp.sum(gain, axis=1, keepdims=True)
    stack = jnp.concatenate([high, low, jnp.ones((16, feats), F32)], axis=0).astype(BF)
    stack_ref[...] = stack
    gsum_ref[...] = jnp.broadcast_to(gain_sum, gsum_ref.shape)
    copies[2].wait()
    frame_sums(hid[...], stack, gain_sum, core, give_ref)
    copies[3].wait()


def project_own_kernel(hid_ref, stack_ref, gsum_ref, own_ref):
    frame_sums(
        hid_ref[...], stack_ref[...], gsum_ref[:, 0:1], lax.axis_index("seq") & 1, own_ref
    )


def project(hidden, head_weight, scale):
    _, feats, tokens = hidden.shape
    rows = tokens // TOK_W
    wide = min(head_weight.shape[1], (feats + 127) // 128 * 128 + 128)
    hbm = pl.BlockSpec(memory_space=pltpu.HBM)
    vmem = pl.BlockSpec(memory_space=pltpu.VMEM)
    sums = jax.ShapeDtypeStruct((rows, HALF + 2 * STAT, 128), BF)
    params = pltpu.CompilerParams(vmem_limit_bytes=16 << 20)
    give, frame, stack, gsum = pl.pallas_call(
        project_give_kernel,
        in_specs=[hbm, hbm, hbm],
        out_specs=[vmem] * 4,
        out_shape=[
            sums,
            jax.ShapeDtypeStruct((feats, tokens), BF),
            jax.ShapeDtypeStruct((144, feats), BF),
            jax.ShapeDtypeStruct((64, 128), F32),
        ],
        scratch_shapes=[
            pltpu.VMEM((feats, tokens), BF),
            pltpu.VMEM((64, wide), F32),
            pltpu.VMEM((1, wide), F32),
            pltpu.SemaphoreType.DMA((4,)),
        ],
        compiler_params=params,
        name="project_give",
    )(in_hbm(hidden), in_hbm(head_weight), in_hbm(scale))

    own = pl.pallas_call(
        project_own_kernel,
        in_specs=[vmem, vmem, vmem],
        out_specs=vmem,
        out_shape=sums,
        compiler_params=params,
        cost_estimate=pl.CostEstimate(
            flops=2 * 144 * feats * tokens, bytes_accessed=1_300_000, transcendentals=0
        ),
        name="project_own",
    )(frame, stack, gsum)
    return own, give


def prepare_first(cin_ref, cin_out):
    zero16 = jnp.zeros((16, 384), BF)
    for tap in range(2):
        for ly in range(4):
            for lx in range(4):
                row = (ly // 2) * 128 + lx * 32 + (ly % 2) * 16
                for qy in range(2):
                    for qx in range(2):
                        dy, dx = ly - qy, lx - qx
                        good = 0 <= dy < 3 and 0 <= dx < 3
                        piece = cin_ref[tap + 1, dy, dx] if good else zero16
                        col = (qy * 2 + qx) * 384
                        cin_out[tap, row : row + 16, col : col + 384] = piece


def prepare_up(up_ref, up_out):
    taps = {(0, 0): (0, 1), (0, 1): (2,), (1, 0): (0,), (1, 1): (1, 2)}
    for dx in range(2):
        for dy in range(2):
            for py in range(2):
                for px in range(2):
                    total = None
                    for b in taps[py, dy]:
                        for e in taps[px, dx]:
                            term = up_ref[b, e].astype(F32)
                            total = term if total is None else total + term
                    total = total.astype(BF)
                    k = slice((dy * 2 + dx) * 384, (dy * 2 + dx + 1) * 384)
                    n = py * 384
                    up_out[n + px * 128 : n + px * 128 + 128, k] = total[0:128]
                    up_out[n + 256 + px * 64 : n + 320 + px * 64, k] = total[128:192]


def prepare_last(cout_ref, cout_out):
    cout_out[...] = jnp.zeros(cout_out.shape, BF)
    for tap in range(2):
        for b in range(3):
            for v in range(2):
                for s in range(2):
                    for o in range(2):
                        e = 2 * v + s - o
                        if not 0 <= e < 3:
                            continue
                        row = b * 768 + v * 384
                        weight = cout_ref[tap + 1, b, e]
                        lo = row + s * 128
                        hi = row + 256 + s * 64
                        cout_out[tap, lo : lo + 128, o * 128 : o * 128 + 96] = weight[0:128]
                        cout_out[tap, hi : hi + 64, o * 128 : o * 128 + 96] = weight[128:192]


def prepare_kernel(
    w_ref, scale_ref, shift_ref, hb_ref, dev_ref, cin_ref, up_ref, upv_ref, cout_ref,
    table_ref, const_ref, cin_out, up_out, upv_out, cout_out, w, cin, up, cout, sems,
):
    copies = [
        pltpu.make_async_copy(source, target, sems.at[i])
        for i, (source, target) in enumerate(
            ((cin_ref, cin), (up_ref, up), (cout_ref, cout), (w_ref, w))
        )
    ]
    for copy in copies:
        copy.start()
    copies[0].wait()
    prepare_first(cin, cin_out)
    copies[1].wait()
    prepare_up(up, up_out)
    vec = upv_ref[...]
    upv_out[...] = jnp.concatenate(
        [vec[:, 0:128], vec[:, 0:128], vec[:, 128:192], vec[:, 128:192]], axis=1
    )
    copies[2].wait()
    prepare_last(cout, cout_out)
    copies[3].wait()
    feats = w_ref.shape[1] // dev_ref.shape[0]
    head = w[...]
    head = jnp.concatenate([head[0:16], head[32:48], head[16:32], head[48:64]], axis=0)
    gain = head * (1.0 + scale_ref[...])
    count = dev_ref.shape[0]
    place = lax.broadcasted_iota(jnp.int32, (count, w_ref.shape[1]), 1) - dev_ref[...] * feats
    inside = ((place >= 0) & (place < feats)).astype(F32)
    dims = (((1,), (1,)), ((), ()))
    sums = lax.dot_general(inside, gain, dims, precision=HIGH, preferred_element_type=F32)
    table_ref[...] = jnp.concatenate([sums, sums], axis=1)
    const = lax.dot_general(
        shift_ref[...], head, dims, precision=HIGH, preferred_element_type=F32
    )
    hb = hb_ref[...]
    hb = jnp.concatenate([hb[:, 0:16], hb[:, 32:48], hb[:, 16:32], hb[:, 48:64]], axis=1)
    const = const + hb
    const_ref[...] = jnp.concatenate([const, const], axis=1)


def prepare(head_weight, mod_scale, mod_shift, head_bias, devs, cin, up, upv, cout):
    count = devs.shape[0]
    hbm = pl.BlockSpec(memory_space=pltpu.HBM)
    vmem = pl.BlockSpec(memory_space=pltpu.VMEM)
    return pl.pallas_call(
        prepare_kernel,
        in_specs=[hbm, vmem, vmem, vmem, vmem, hbm, hbm, vmem, hbm],
        scratch_shapes=[
            pltpu.VMEM(head_weight.shape, F32),
            pltpu.VMEM(cin.shape, BF),
            pltpu.VMEM(up.shape, BF),
            pltpu.VMEM(cout.shape, BF),
            pltpu.SemaphoreType.DMA((4,)),
        ],
        out_shape=[
            jax.ShapeDtypeStruct((count, 128), F32),
            jax.ShapeDtypeStruct((1, 128), F32),
            jax.ShapeDtypeStruct((2, 256, 1536), BF),
            jax.ShapeDtypeStruct((768, 1536), BF),
            jax.ShapeDtypeStruct((2, 384), F32),
            jax.ShapeDtypeStruct((2, 2304, 256), BF),
        ],
        compiler_params=pltpu.CompilerParams(vmem_limit_bytes=20 << 20),
        cost_estimate=pl.CostEstimate(
            flops=20_000_000, bytes_accessed=10_000_000, transcendentals=0
        ),
        name="prepare",
    )(
        in_hbm(head_weight), mod_scale, mod_shift, head_bias, devs, in_hbm(cin), in_hbm(up), upv,
        in_hbm(cout),
    )


def silu_half(half):
    return half + half * jnp.tanh(half)


def decode_kernel(
    group, flags_ref, own_ref, near_ref, core_ref, far_ref, table_ref, const_ref, cin_ref, cinv_ref, up_ref, upv_ref, cout_ref,
    coutv_ref, out_ref, fa, fb, fx, ua, ub, xe, xo, lines, outs, sems,
):
    count = table_ref.shape[0]

    def flagged(row, value):
        return jnp.broadcast_to(flags_ref[row : row + 1, 0 : value.shape[1]], value.shape) > 0.5

    def choose(row, yes, no):
        return jnp.where(flagged(row, yes), yes, no)

    n_stat = 2 * (own_ref.shape[1] - HALF)

    pick_row = lax.broadcasted_iota(jnp.int32, (count + 8, n_stat), 0)
    pick_col = lax.broadcasted_iota(jnp.int32, (count + 8, n_stat), 1)
    of_dev, of_kind = pick_col // STAT, pick_col % STAT
    pick = ((of_kind < 2) & (pick_row == of_dev)) | ((of_kind >= 2) & (pick_row == count))
    pick = pick.astype(F32).astype(BF)
    lane40 = lanes(HALF)
    lane80, sub80 = lanes(TOK_W), lax.broadcasted_iota(jnp.int32, (TOK_W, 128), 0)
    loaded = [r[...].astype(F32) for r in (own_ref, near_ref, core_ref, far_ref)]
    wide = []
    for j in range(3):
        mine, other = [
            jnp.concatenate([a[j, HALF:], b[j, HALF:]], axis=0) for a, b in (loaded[:2], loaded[2:])
        ]
        wide += [choose(0, mine, other), choose(0, other, mine)]
    wide = jnp.concatenate(wide, axis=1).astype(BF)
    stats = jnp.dot(pick, wide, preferred_element_type=F32)
    means = stats[0:count]
    off = means - jnp.sum(means, axis=0, keepdims=True) * (1.0 / count)
    var = stats[count : count + 1] + group * jnp.sum(off * off, axis=0, keepdims=True)
    inv = lax.rsqrt(var * (1.0 / (count * group)) + EPS)
    off_hi, off_lo = split(off)
    inv_hi, inv_lo = split(inv)
    left = jnp.concatenate(
        [off_hi, off_lo, off_hi, inv_hi, inv_lo, jnp.zeros((14, off.shape[1]), F32)], axis=0
    )
    tab_hi, tab_lo = split(table_ref[...])
    right = jnp.concatenate(
        [
            jnp.concatenate([tab_hi, tab_hi, tab_lo, jnp.zeros((16, 128), F32)], axis=0),
            jnp.concatenate(
                [
                    jnp.zeros((3 * count, 128), F32),
                    jnp.ones((2, 128), F32),
                    jnp.zeros((14, 128), F32),
                ],
                axis=0,
            ),
        ],
        axis=1,
    )
    per_token = jnp.dot(left.T.astype(BF), right.astype(BF), preferred_element_type=F32)
    edge = [[None] * 3 for _ in range(2)]
    first_lanes = jnp.concatenate([lane40, lane40], axis=1) % 128 < 64
    for j in range(3):
        mine, other = [
            a[j, 0:HALF] + b[j, 0:HALF] for a, b in (loaded[:2], loaded[2:])
        ]
        sums = [choose(0, mine, other), choose(0, other, mine)]
        for f in range(2):
            at = (j * 2 + f) * 128
            token = jnp.where(
                first_lanes, per_token[at : at + HALF], per_token[at + 64 : at + 64 + HALF]
            )
            row = (sums[f] + token[:, 0:128]) * token[:, 128:256] + const_ref[...]
            if j == 0:
                row = choose(1, row, 0.0)
            if j == 2:
                row = choose(2, row, 0.0)
            swapped = pltpu.roll(row, 64, 1)
            both = jnp.concatenate(
                [jnp.where(lane40 < 64, row, swapped), jnp.where(lane40 < 64, swapped, row)],
                axis=0,
            )
            both = pltpu.roll(both, 32, 1)
            before = jnp.where(sub80 == 0, 0.0, pltpu.roll(both, 1, 0))
            after = jnp.where(sub80 == TOK_W - 1, 0.0, pltpu.roll(both, TOK_W - 1, 0))
            edge[f][j] = jnp.where(
                lane80 < 32, before, jnp.where(lane80 >= 96, after, both)
            ).astype(BF)

    def patch(f):
        return jnp.concatenate(
            [jnp.concatenate([edge[f][b], edge[f][b + 1]], axis=1) for b in range(2)], axis=0
        )

    patches = [patch(0), patch(1)]
    both, late = [], []
    for n in range(2):
        cols = slice(n * 768, n * 768 + 768)
        both.append(jnp.dot(jnp.concatenate(patches, axis=0), cin_ref[1, :, cols], preferred_element_type=F32))
        late.append(jnp.dot(patches[0], cin_ref[0, :, cols], preferred_element_type=F32))
    both = jnp.concatenate(both, axis=1)
    pres = [both[0 : 2 * TOK_W], both[2 * TOK_W :] + jnp.concatenate(late, axis=1)]
    bias_in, gain_in = cinv_ref[0:1], cinv_ref[1:2] * 0.5
    sub_one = lax.broadcasted_iota(jnp.int32, (TOK_W, 384), 0)
    zeros_ext = jnp.zeros((TOK_W, 384), F32)
    for f in range(2):
        pre = pres[f]
        for b in range(2):
            for qy in range(2):
                y = 2 * b + qy
                act = []
                for qx in range(2):
                    col = (qy * 2 + qx) * 384
                    v = pre[b * TOK_W : (b + 1) * TOK_W, col : col + 384] + bias_in
                    mean_sq = jnp.sum(v * v, axis=1, keepdims=True) * (1.0 / 384)
                    a = silu_half(v * lax.rsqrt(mean_sq + EPS) * gain_in)
                    if y == 0:
                        a = choose(1, a, 0.0)
                    if y == 3:
                        a = choose(2, a, 0.0)
                    act.append(a)
                even, odd = act
                back = jnp.where(sub_one == 0, 0.0, pltpu.roll(odd, 1, 0))
                even, odd, back = even.astype(BF), odd.astype(BF), back.astype(BF)
                for pair, part in ((y - 1, 1), (y, 0)):
                    if not 0 <= pair < 3:
                        continue
                    at = slice((f * 3 + pair) * TOK_W, (f * 3 + pair + 1) * TOK_W)
                    fa[at, part * 768 : part * 768 + 384] = even
                    fa[at, part * 768 + 384 : part * 768 + 768] = odd
                    fb[at, part * 768 : part * 768 + 384] = back
                    fb[at, part * 768 + 384 : part * 768 + 768] = even
                    fx[f * 3 + pair : f * 3 + pair + 1, part * 768 : part * 768 + 384] = act[1][
                        TOK_W - 1 : TOK_W
                    ]
                    fx[f * 3 + pair : f * 3 + pair + 1, part * 768 + 384 : part * 768 + 768] = (
                        zeros_ext[0:1]
                    )
    del sub_one

    extra_in = jnp.where(
        lax.broadcasted_iota(jnp.int32, (8, 1536), 0) < 6, fx[...], 0.0
    )
    extra_in = jnp.concatenate([extra_in, jnp.zeros((8, 1536), F32)], axis=0).astype(BF)
    fb[6 * TOK_W :] = extra_in
    chunk = 3 * TOK_W
    for n in range(0, 768, 256):
        for first in (0, chunk):
            for given, result in ((fa, ua), (fb, ub)):
                rows = slice(first, first + chunk if first == 0 else given.shape[0])
                result[rows, n : n + 256] = lax.dot_general(
                    given[rows], up_ref[n : n + 256], (((1,), (1,)), ((), ())),
                    preferred_element_type=F32,
                )
    extra = ub[6 * TOK_W : 6 * TOK_W + 8]
    bias_up, gain_up = upv_ref[0:1], upv_ref[1:2] * 0.5

    def second(u):
        v = u + bias_up
        t0, t1, t2 = v[:, 0:128], v[:, 128:256], v[:, 256:384]
        lane = lanes(u.shape[0])
        q = t2 * t2
        left = jnp.sum(t0 * t0 + jnp.where(lane < 64, q, 0.0), axis=1, keepdims=True)
        right = jnp.sum(t1 * t1 + jnp.where(lane < 64, 0.0, q), axis=1, keepdims=True)
        left = lax.rsqrt(left * (1.0 / 192) + EPS)
        right = lax.rsqrt(right * (1.0 / 192) + EPS)
        g = gain_up
        return (
            silu_half(t0 * left * g[:, 0:128]),
            silu_half(t1 * right * g[:, 128:256]),
            silu_half(t2 * jnp.where(lane < 64, left, right) * g[:, 256:384]),
        )

    ends = [second(extra[:, py * 384 : py * 384 + 384]) for py in range(2)]
    for f in range(2):
        for pair in range(3):
            at = (f * 3 + pair) * TOK_W
            for py in range(2):
                y = pair * 2 + py
                cols = slice(py * 384, py * 384 + 384)

                def keep(value, y=y):
                    if y == 0:
                        return choose(1, value, 0.0)
                    if y == 5:
                        return choose(2, value, 0.0)
                    return value

                mid = [keep(t) for t in second(ua[at : at + TOK_W, cols])]
                low = [keep(t) for t in second(ub[at : at + TOK_W, cols])]
                end = [keep(t) for t in ends[py]]
                to = slice(y * TOK_W, (y + 1) * TOK_W)
                first = sub80 == 0
                low[0] = jnp.where(first, 0.0, low[0])
                low[2] = jnp.where(first & (lane80 < 64), 0.0, low[2])
                end[1] = jnp.zeros_like(end[1])
                end[2] = jnp.where(lanes(8) < 64, end[2], 0.0)
                for k in range(3):
                    m = mid[k].astype(BF)
                    xe[f, to, k * 128 : k * 128 + 128] = low[k].astype(BF)
                    xe[f, to, 384 + k * 128 : 512 + k * 128] = m
                    xo[f, to, k * 128 : k * 128 + 128] = m
                    last = end[k][f * 3 + pair : f * 3 + pair + 1]
                    ahead = jnp.where(
                        sub80 == TOK_W - 1, last, pltpu.roll(low[k], TOK_W - 1, 0)
                    )
                    xo[f, to, 384 + k * 128 : 512 + k * 128] = ahead.astype(BF)

    bias_out = coutv_ref[...]
    copies = []
    for f in range(2):
        for side, x in enumerate((xe, xo)):
            acc = None
            for b in range(3):
                rows = slice(b * TOK_W, (b + 4) * TOK_W)
                ks = slice(b * 768, b * 768 + 768)
                term = jnp.dot(x[f, rows], cout_ref[1, ks], preferred_element_type=F32)
                acc = term if acc is None else acc + term
                if f == 1:
                    acc = acc + jnp.dot(x[0, rows], cout_ref[0, ks], preferred_element_type=F32)
            for j in range(4):
                for o in range(2):
                    lines[f, j, pl.ds(2 * side + o, TOK_W, stride=4), :] = (
                        acc[j * TOK_W : (j + 1) * TOK_W, o * 128 : o * 128 + 128] + bias_out
                    )
        for j in range(4):
            outs[f, j] = lines[f, j].T[0:96].astype(BF)
        copy = pltpu.make_async_copy(outs.at[f], out_ref.at[f], sems.at[f])
        copy.start()
        copies.append(copy)
    for copy in copies:
        copy.wait()


def decode(group, flags, pieces, table, const, cin, cinv, up, upv, cout, coutv):
    vmem = pl.BlockSpec(memory_space=pltpu.VMEM)
    return pl.pallas_call(
        functools.partial(decode_kernel, float(group)),
        in_specs=[vmem] * 13,
        out_specs=pl.BlockSpec(memory_space=pltpu.HBM),
        out_shape=jax.ShapeDtypeStruct((2, 4, 96, 4 * TOK_W), BF),
        scratch_shapes=[
            pltpu.VMEM((6 * TOK_W, 1536), BF),
            pltpu.VMEM((6 * TOK_W + 16, 1536), BF),
            pltpu.VMEM((8, 1536), F32),
            pltpu.VMEM((6 * TOK_W, 768), F32),
            pltpu.VMEM((6 * TOK_W + 16, 768), F32),
            pltpu.VMEM((2, 6 * TOK_W, 768), BF),
            pltpu.VMEM((2, 6 * TOK_W, 768), BF),
            pltpu.VMEM((2, 4, 4 * TOK_W, 128), F32),
            pltpu.VMEM((2, 4, 96, 4 * TOK_W), BF),
            pltpu.SemaphoreType.DMA((2,)),
        ],
        compiler_params=pltpu.CompilerParams(vmem_limit_bytes=24 << 20),
        cost_estimate=pl.CostEstimate(
            flops=5_000_000_000, bytes_accessed=8_000_000, transcendentals=1_300_000
        ),
        name="decode",
    )(flags, *pieces, table, const, cin, cinv, up, upv, cout, coutv)


def exchange(block, mask, count):
    return lax.ppermute(block, "seq", [(i, i ^ mask) for i in range(count)])


def merged(own, received):
    total = own[:, :HALF].astype(F32)
    for item in received:
        total = total + item[:, :HALF].astype(F32)
    return jnp.concatenate(
        [total.astype(BF), own[:, HALF:]] + [item[:, HALF:] for item in received], axis=1
    )


def cut(block, start, size):
    return lax.dynamic_slice_in_dim(block, start, size, 0)


def steps_of(count):
    bit = count.bit_length() - 3
    steps = [[2 << bit, 1 << bit, 3 << bit]]
    while bit > 2:
        bit -= 1
        steps.append([1 << bit])
    return steps


def device_order(count):
    order = [0]
    for masks in steps_of(count):
        order = order + [o ^ mask for mask in masks for o in order]
    order = order + [o ^ 2 for o in order]
    return np.asarray([o + c for o in order for c in range(2)], np.int32)


def gather_rows(own, give, weights, ready, me, count):
    block = (own.astype(F32) + exchange(give, 1, count).astype(F32)).astype(BF)
    block, weights = lax.optimization_barrier((block, weights))

    def window(base, size):
        return jnp.clip(base - 1, 0, count - size)

    start = jnp.int32(0)
    for masks in steps_of(count):
        unit = min(masks)
        size = unit + 2
        base = (me // unit) * unit
        new = window(base, size)
        received = [
            exchange(cut(block, window(base ^ mask, size) - start, size), mask, count)
            for mask in masks
        ]
        block = merged(cut(block, new - start, size), received)
        if len(masks) > 1:
            block, weights = lax.optimization_barrier((block, ready(weights)))
        start = new
    padded = jnp.pad(block, ((1, 1), (0, 0), (0, 0)))
    pieces = [cut(padded, me - start, 3)]
    for mask in (2, 1, 3):
        pieces.append(exchange(cut(padded, (me ^ mask) - start, 3), mask, count))
    return pieces, weights


def local(
    hidden,
    mod_shift,
    mod_scale,
    head_weight,
    head_bias,
    conv_in_weight,
    conv_in_bias,
    gain_in,
    up_weight,
    up_bias,
    gain_up,
    out_weight,
    out_bias,
):
    count = lax.axis_size("seq")
    me = lax.axis_index("seq")
    feats = hidden.shape[1]
    flags = jnp.stack([me % 2 == 0, me > 0, me < count - 1]).astype(F32)
    flags = jnp.broadcast_to(flags[:, None], (3, 384))
    own, give = project(hidden, head_weight, mod_scale[None])
    weights = (head_weight, conv_in_weight, jnp.swapaxes(up_weight, 2, 3), out_weight)

    def ready(parts):
        head_again, cin, up, cout = parts
        return flags, prepare(
            head_again, mod_scale[None], mod_shift[None], head_bias[None],
            (((me // 2) * 2) ^ device_order(count))[:, None],
            cin, up, jnp.stack([up_bias, gain_up]), cout,
        )

    pieces, weights = gather_rows(own, give, weights, ready, me, count)
    flags, (table, const, cin, up, upv, cout) = weights
    cinv = jnp.stack([conv_in_bias, gain_in])
    coutv = jnp.pad(out_bias, (0, 32))[None]
    out = decode(feats, flags, pieces, table, const, cin, cinv, up, upv, cout, coutv)
    return jnp.swapaxes(out, 2, 3)


def solution(mesh):
    placed = (P("grp", "seq", None), P(), P(), P(), P(), P(), P(), P(), P(), P(), P(), P(), P())
    return jax.shard_map(
        local, mesh=mesh, in_specs=placed, out_specs=P("grp", "seq", None, None), check_vma=False
    )
```

```python
import functools
import jax
import jax.numpy as jnp
import numpy as np
from jax import lax
from jax.experimental import pallas as pl
from jax.experimental.pallas import tpu as pltpu
from jax.sharding import PartitionSpec as P

TOK_W = 80
HALF = TOK_W // 2
STAT = 4
EPS = 1e-06
HIGH = lax.Precision.HIGHEST
BF = jnp.bfloat16
F32 = jnp.float32


def in_hbm(value):
    return pltpu.with_memory_space_constraint(value, pltpu.HBM)


def split(values):
    high = values.astype(BF).astype(F32)
    return high, values - high


def lanes(rows):
    return lax.broadcasted_iota(jnp.int32, (rows, 128), 1)


def frame_sums(x, stack, gain_sum, core, out_ref):
    feats, tokens = x.shape
    width = 640
    lane40 = lanes(HALF)
    lane = lanes(8)
    sub = lax.broadcasted_iota(jnp.int32, (8, 128), 0)
    for i in range(tokens // width):
        block = x[:, i * width : (i + 1) * width]
        prod = jnp.dot(stack, block, preferred_element_type=F32)
        mean = prod[128:129] * (1.0 / feats)
        part = prod[0:64] + prod[64:128] - gain_sum * mean
        off = block.astype(F32) - mean
        second = jnp.sum(off * off, axis=0, keepdims=True)
        m_hi, m_lo = split(mean)
        s_hi, s_lo = split(second)
        stats = jnp.concatenate([m_hi, m_lo, s_hi, s_lo] * 2, axis=0)
        flat = jnp.concatenate([part, part], axis=0).T
        for row in range(width // TOK_W):
            first = row * TOK_W
            sums = jnp.where(
                lane40 < 64, flat[first : first + HALF], flat[first + HALF : first + TOK_W]
            )
            picks = []
            for h in range(2):
                at = first + h * HALF
                base = (at // 128) * 128
                span = min(256, width - base)
                window = stats[:, base : base + span]
                shift = (64 * h - (at - base)) % span
                if shift:
                    window = pltpu.roll(window, shift, 1)
                picks.append(window[:, :128])
            tail = jnp.where(
                lane < HALF,
                picks[0],
                jnp.where((lane >= 64) & (lane < 64 + HALF), picks[1], 0.0),
            )
            tail = jnp.where(lax.div(sub, STAT) == core, tail, 0.0)
            out_ref[i * (width // TOK_W) + row] = jnp.concatenate([sums, tail], axis=0).astype(BF)


def project_give_kernel(
    hid_ref, w_ref, scale_ref, give_ref, own_ref, stack_ref, gsum_ref,
    hid, w, scale, sems,
):
    feats = hid_ref.shape[1]
    me = lax.axis_index("seq")
    core = me & 1
    wide = w.shape[1]
    at = jnp.minimum(lax.div(me * feats, 128) * 128, w_ref.shape[1] - wide)
    at = pl.multiple_of(at, 128)
    copies = [
        pltpu.make_async_copy(w_ref.at[:, pl.ds(at, wide)], w, sems.at[0]),
        pltpu.make_async_copy(scale_ref.at[:, pl.ds(at, wide)], scale, sems.at[1]),
        pltpu.make_async_copy(hid_ref.at[1 - core], hid, sems.at[2]),
        pltpu.make_async_copy(hid_ref.at[core], own_ref, sems.at[3]),
    ]
    for copy in copies:
        copy.start()
    copies[0].wait()
    copies[1].wait()
    gain = w[...] * (1.0 + scale[...])
    gain = pltpu.roll(gain, wide - (me * feats - at), 1)[:, :feats]
    gain = jnp.concatenate([gain[0:16], gain[32:48], gain[16:32], gain[48:64]], axis=0)
    high, low = split(gain)
    gain_sum = jnp.sum(gain, axis=1, keepdims=True)
    stack = jnp.concatenate([high, low, jnp.ones((16, feats), F32)], axis=0).astype(BF)
    stack_ref[...] = stack
    gsum_ref[...] = jnp.broadcast_to(gain_sum, gsum_ref.shape)
    copies[2].wait()
    frame_sums(hid[...], stack, gain_sum, core, give_ref)
    copies[3].wait()


def project_own_kernel(hid_ref, stack_ref, gsum_ref, own_ref):
    frame_sums(
        hid_ref[...], stack_ref[...], gsum_ref[:, 0:1], lax.axis_index("seq") & 1, own_ref
    )


def project(hidden, head_weight, scale):
    _, feats, tokens = hidden.shape
    rows = tokens // TOK_W
    wide = min(head_weight.shape[1], (feats + 127) // 128 * 128 + 128)
    hbm = pl.BlockSpec(memory_space=pltpu.HBM)
    vmem = pl.BlockSpec(memory_space=pltpu.VMEM)
    sums = jax.ShapeDtypeStruct((rows, HALF + 2 * STAT, 128), BF)
    params = pltpu.CompilerParams(vmem_limit_bytes=16 << 20)
    give, frame, stack, gsum = pl.pallas_call(
        project_give_kernel,
        in_specs=[hbm, hbm, hbm],
        out_specs=[vmem] * 4,
        out_shape=[
            sums,
            jax.ShapeDtypeStruct((feats, tokens), BF),
            jax.ShapeDtypeStruct((144, feats), BF),
            jax.ShapeDtypeStruct((64, 128), F32),
        ],
        scratch_shapes=[
            pltpu.VMEM((feats, tokens), BF),
            pltpu.VMEM((64, wide), F32),
            pltpu.VMEM((1, wide), F32),
            pltpu.SemaphoreType.DMA((4,)),
        ],
        compiler_params=params,
        name="project_give",
    )(in_hbm(hidden), in_hbm(head_weight), in_hbm(scale))

    own = pl.pallas_call(
        project_own_kernel,
        in_specs=[vmem, vmem, vmem],
        out_specs=vmem,
        out_shape=sums,
        compiler_params=params,
        cost_estimate=pl.CostEstimate(
            flops=2 * 144 * feats * tokens, bytes_accessed=1_300_000, transcendentals=0
        ),
        name="project_own",
    )(frame, stack, gsum)
    return own, give


def prepare_first(cin_ref, cin_out):
    zero16 = jnp.zeros((16, 384), BF)
    for tap in range(2):
        for ly in range(4):
            for lx in range(4):
                row = (ly // 2) * 128 + lx * 32 + (ly % 2) * 16
                for qy in range(2):
                    for qx in range(2):
                        dy, dx = ly - qy, lx - qx
                        good = 0 <= dy < 3 and 0 <= dx < 3
                        piece = cin_ref[tap + 1, dy, dx] if good else zero16
                        col = (qy * 2 + qx) * 384
                        cin_out[tap, row : row + 16, col : col + 384] = piece


def prepare_up(up_ref, up_out):
    taps = {(0, 0): (0, 1), (0, 1): (2,), (1, 0): (0,), (1, 1): (1, 2)}
    for dx in range(2):
        for dy in range(2):
            for py in range(2):
                for px in range(2):
                    total = None
                    for b in taps[py, dy]:
                        for e in taps[px, dx]:
                            term = up_ref[b, e].astype(F32)
                            total = term if total is None else total + term
                    total = total.astype(BF)
                    k = slice((dy * 2 + dx) * 384, (dy * 2 + dx + 1) * 384)
                    n = py * 384
                    up_out[n + px * 128 : n + px * 128 + 128, k] = total[0:128]
                    up_out[n + 256 + px * 64 : n + 320 + px * 64, k] = total[128:192]


def prepare_last(cout_ref, cout_out):
    cout_out[...] = jnp.zeros(cout_out.shape, BF)
    for tap in range(2):
        for b in range(3):
            for v in range(2):
                for s in range(2):
                    for o in range(2):
                        e = 2 * v + s - o
                        if not 0 <= e < 3:
                            continue
                        row = b * 768 + v * 384
                        weight = cout_ref[tap + 1, b, e]
                        lo = row + s * 128
                        hi = row + 256 + s * 64
                        cout_out[tap, lo : lo + 128, o * 128 : o * 128 + 96] = weight[0:128]
                        cout_out[tap, hi : hi + 64, o * 128 : o * 128 + 96] = weight[128:192]


def prepare_kernel(
    w_ref, scale_ref, shift_ref, hb_ref, dev_ref, cin_ref, up_ref, upv_ref, cout_ref,
    table_ref, const_ref, cin_out, up_out, upv_out, cout_out, w, cin, up, cout, sems,
):
    copies = [
        pltpu.make_async_copy(source, target, sems.at[i])
        for i, (source, target) in enumerate(
            ((cin_ref, cin), (up_ref, up), (cout_ref, cout), (w_ref, w))
        )
    ]
    for copy in copies:
        copy.start()
    copies[0].wait()
    prepare_first(cin, cin_out)
    copies[1].wait()
    prepare_up(up, up_out)
    vec = upv_ref[...]
    upv_out[...] = jnp.concatenate(
        [vec[:, 0:128], vec[:, 0:128], vec[:, 128:192], vec[:, 128:192]], axis=1
    )
    copies[2].wait()
    prepare_last(cout, cout_out)
    copies[3].wait()
    feats = w_ref.shape[1] // dev_ref.shape[0]
    head = w[...]
    head = jnp.concatenate([head[0:16], head[32:48], head[16:32], head[48:64]], axis=0)
    gain = head * (1.0 + scale_ref[...])
    count = dev_ref.shape[0]
    place = lax.broadcasted_iota(jnp.int32, (count, w_ref.shape[1]), 1) - dev_ref[...] * feats
    inside = ((place >= 0) & (place < feats)).astype(F32)
    dims = (((1,), (1,)), ((), ()))
    sums = lax.dot_general(inside, gain, dims, precision=HIGH, preferred_element_type=F32)
    table_ref[...] = jnp.concatenate([sums, sums], axis=1)
    const = lax.dot_general(
        shift_ref[...], head, dims, precision=HIGH, preferred_element_type=F32
    )
    hb = hb_ref[...]
    hb = jnp.concatenate([hb[:, 0:16], hb[:, 32:48], hb[:, 16:32], hb[:, 48:64]], axis=1)
    const = const + hb
    const_ref[...] = jnp.concatenate([const, const], axis=1)


def prepare(head_weight, mod_scale, mod_shift, head_bias, devs, cin, up, upv, cout):
    count = devs.shape[0]
    hbm = pl.BlockSpec(memory_space=pltpu.HBM)
    vmem = pl.BlockSpec(memory_space=pltpu.VMEM)
    return pl.pallas_call(
        prepare_kernel,
        in_specs=[hbm, vmem, vmem, vmem, vmem, hbm, hbm, vmem, hbm],
        scratch_shapes=[
            pltpu.VMEM(head_weight.shape, F32),
            pltpu.VMEM(cin.shape, BF),
            pltpu.VMEM(up.shape, BF),
            pltpu.VMEM(cout.shape, BF),
            pltpu.SemaphoreType.DMA((4,)),
        ],
        out_shape=[
            jax.ShapeDtypeStruct((count, 128), F32),
            jax.ShapeDtypeStruct((1, 128), F32),
            jax.ShapeDtypeStruct((2, 256, 1536), BF),
            jax.ShapeDtypeStruct((768, 1536), BF),
            jax.ShapeDtypeStruct((2, 384), F32),
            jax.ShapeDtypeStruct((2, 2304, 256), BF),
        ],
        compiler_params=pltpu.CompilerParams(vmem_limit_bytes=20 << 20),
        cost_estimate=pl.CostEstimate(
            flops=20_000_000, bytes_accessed=10_000_000, transcendentals=0
        ),
        name="prepare",
    )(
        in_hbm(head_weight), mod_scale, mod_shift, head_bias, devs, in_hbm(cin), in_hbm(up), upv,
        in_hbm(cout),
    )


def silu_half(half):
    return half + half * jnp.tanh(half)


def decode_kernel(
    group, flags_ref, own_ref, near_ref, core_ref, far_ref, table_ref, const_ref, cin_ref, cinv_ref, up_ref, upv_ref, cout_ref,
    coutv_ref, out_ref, fa, fb, fx, ua, ub, xe, xo, lines, outs, sems,
):
    count = table_ref.shape[0]

    def flagged(row, value):
        return jnp.broadcast_to(flags_ref[row : row + 1, 0 : value.shape[1]], value.shape) > 0.5

    def choose(row, yes, no):
        return jnp.where(flagged(row, yes), yes, no)

    n_stat = 2 * (own_ref.shape[1] - HALF)

    pick_row = lax.broadcasted_iota(jnp.int32, (count + 8, n_stat), 0)
    pick_col = lax.broadcasted_iota(jnp.int32, (count + 8, n_stat), 1)
    of_dev, of_kind = pick_col // STAT, pick_col % STAT
    pick = ((of_kind < 2) & (pick_row == of_dev)) | ((of_kind >= 2) & (pick_row == count))
    pick = pick.astype(F32).astype(BF)
    lane40 = lanes(HALF)
    lane80, sub80 = lanes(TOK_W), lax.broadcasted_iota(jnp.int32, (TOK_W, 128), 0)
    loaded = [r[...].astype(F32) for r in (own_ref, near_ref, core_ref, far_ref)]
    wide = []
    for j in range(3):
        mine, other = [
            jnp.concatenate([a[j, HALF:], b[j, HALF:]], axis=0) for a, b in (loaded[:2], loaded[2:])
        ]
        wide += [choose(0, mine, other), choose(0, other, mine)]
    wide = jnp.concatenate(wide, axis=1).astype(BF)
    stats = jnp.dot(pick, wide, preferred_element_type=F32)
    means = stats[0:count]
    off = means - jnp.sum(means, axis=0, keepdims=True) * (1.0 / count)
    var = stats[count : count + 1] + group * jnp.sum(off * off, axis=0, keepdims=True)
    inv = lax.rsqrt(var * (1.0 / (count * group)) + EPS)
    off_hi, off_lo = split(off)
    inv_hi, inv_lo = split(inv)
    left = jnp.concatenate(
        [off_hi, off_lo, off_hi, inv_hi, inv_lo, jnp.zeros((14, off.shape[1]), F32)], axis=0
    )
    tab_hi, tab_lo = split(table_ref[...])
    right = jnp.concatenate(
        [
            jnp.concatenate([tab_hi, tab_hi, tab_lo, jnp.zeros((16, 128), F32)], axis=0),
            jnp.concatenate(
                [
                    jnp.zeros((3 * count, 128), F32),
                    jnp.ones((2, 128), F32),
                    jnp.zeros((14, 128), F32),
                ],
                axis=0,
            ),
        ],
        axis=1,
    )
    per_token = jnp.dot(left.T.astype(BF), right.astype(BF), preferred_element_type=F32)
    edge = [[None] * 3 for _ in range(2)]
    first_lanes = jnp.concatenate([lane40, lane40], axis=1) % 128 < 64
    for j in range(3):
        mine, other = [
            a[j, 0:HALF] + b[j, 0:HALF] for a, b in (loaded[:2], loaded[2:])
        ]
        sums = [choose(0, mine, other), choose(0, other, mine)]
        for f in range(2):
            at = (j * 2 + f) * 128
            token = jnp.where(
                first_lanes, per_token[at : at + HALF], per_token[at + 64 : at + 64 + HALF]
            )
            row = (sums[f] + token[:, 0:128]) * token[:, 128:256] + const_ref[...]
            if j == 0:
                row = choose(1, row, 0.0)
            if j == 2:
                row = choose(2, row, 0.0)
            swapped = pltpu.roll(row, 64, 1)
            both = jnp.concatenate(
                [jnp.where(lane40 < 64, row, swapped), jnp.where(lane40 < 64, swapped, row)],
                axis=0,
            )
            both = pltpu.roll(both, 32, 1)
            before = jnp.where(sub80 == 0, 0.0, pltpu.roll(both, 1, 0))
            after = jnp.where(sub80 == TOK_W - 1, 0.0, pltpu.roll(both, TOK_W - 1, 0))
            edge[f][j] = jnp.where(
                lane80 < 32, before, jnp.where(lane80 >= 96, after, both)
            ).astype(BF)

    def patch(f):
        return jnp.concatenate(
            [jnp.concatenate([edge[f][b], edge[f][b + 1]], axis=1) for b in range(2)], axis=0
        )

    patches = [patch(0), patch(1)]
    both, late = [], []
    for n in range(2):
        cols = slice(n * 768, n * 768 + 768)
        both.append(jnp.dot(jnp.concatenate(patches, axis=0), cin_ref[1, :, cols], preferred_element_type=F32))
        late.append(jnp.dot(patches[0], cin_ref[0, :, cols], preferred_element_type=F32))
    both = jnp.concatenate(both, axis=1)
    pres = [both[0 : 2 * TOK_W], both[2 * TOK_W :] + jnp.concatenate(late, axis=1)]
    bias_in, gain_in = cinv_ref[0:1], cinv_ref[1:2] * 0.5
    sub_one = lax.broadcasted_iota(jnp.int32, (TOK_W, 384), 0)
    zeros_ext = jnp.zeros((TOK_W, 384), F32)
    for f in range(2):
        pre = pres[f]
        for b in range(2):
            for qy in range(2):
                y = 2 * b + qy
                act = []
                for qx in range(2):
                    col = (qy * 2 + qx) * 384
                    v = pre[b * TOK_W : (b + 1) * TOK_W, col : col + 384] + bias_in
                    mean_sq = jnp.sum(v * v, axis=1, keepdims=True) * (1.0 / 384)
                    a = silu_half(v * lax.rsqrt(mean_sq + EPS) * gain_in)
                    if y == 0:
                        a = choose(1, a, 0.0)
                    if y == 3:
                        a = choose(2, a, 0.0)
                    act.append(a)
                even, odd = act
                back = jnp.where(sub_one == 0, 0.0, pltpu.roll(odd, 1, 0))
                even, odd, back = even.astype(BF), odd.astype(BF), back.astype(BF)
                for pair, part in ((y - 1, 1), (y, 0)):
                    if not 0 <= pair < 3:
                        continue
                    at = slice((f * 3 + pair) * TOK_W, (f * 3 + pair + 1) * TOK_W)
                    fa[at, part * 768 : part * 768 + 384] = even
                    fa[at, part * 768 + 384 : part * 768 + 768] = odd
                    fb[at, part * 768 : part * 768 + 384] = back
                    fb[at, part * 768 + 384 : part * 768 + 768] = even
                    fx[f * 3 + pair : f * 3 + pair + 1, part * 768 : part * 768 + 384] = act[1][
                        TOK_W - 1 : TOK_W
                    ]
                    fx[f * 3 + pair : f * 3 + pair + 1, part * 768 + 384 : part * 768 + 768] = (
                        zeros_ext[0:1]
                    )
    del sub_one

    extra_in = jnp.where(
        lax.broadcasted_iota(jnp.int32, (8, 1536), 0) < 6, fx[...], 0.0
    )
    extra_in = jnp.concatenate([extra_in, jnp.zeros((8, 1536), F32)], axis=0).astype(BF)
    fb[6 * TOK_W :] = extra_in
    chunk = 3 * TOK_W
    for n in range(0, 768, 256):
        for first in (0, chunk):
            for given, result in ((fa, ua), (fb, ub)):
                rows = slice(first, first + chunk if first == 0 else given.shape[0])
                result[rows, n : n + 256] = lax.dot_general(
                    given[rows], up_ref[n : n + 256], (((1,), (1,)), ((), ())),
                    preferred_element_type=F32,
                )
    extra = ub[6 * TOK_W : 6 * TOK_W + 8]
    bias_up, gain_up = upv_ref[0:1], upv_ref[1:2] * 0.5

    def second(u):
        v = u + bias_up
        t0, t1, t2 = v[:, 0:128], v[:, 128:256], v[:, 256:384]
        lane = lanes(u.shape[0])
        q = t2 * t2
        left = jnp.sum(t0 * t0 + jnp.where(lane < 64, q, 0.0), axis=1, keepdims=True)
        right = jnp.sum(t1 * t1 + jnp.where(lane < 64, 0.0, q), axis=1, keepdims=True)
        left = lax.rsqrt(left * (1.0 / 192) + EPS)
        right = lax.rsqrt(right * (1.0 / 192) + EPS)
        g = gain_up
        return (
            silu_half(t0 * left * g[:, 0:128]),
            silu_half(t1 * right * g[:, 128:256]),
            silu_half(t2 * jnp.where(lane < 64, left, right) * g[:, 256:384]),
        )

    ends = [second(extra[:, py * 384 : py * 384 + 384]) for py in range(2)]
    for f in range(2):
        for pair in range(3):
            at = (f * 3 + pair) * TOK_W
            for py in range(2):
                y = pair * 2 + py
                cols = slice(py * 384, py * 384 + 384)

                def keep(value, y=y):
                    if y == 0:
                        return choose(1, value, 0.0)
                    if y == 5:
                        return choose(2, value, 0.0)
                    return value

                mid = [keep(t) for t in second(ua[at : at + TOK_W, cols])]
                low = [keep(t) for t in second(ub[at : at + TOK_W, cols])]
                end = [keep(t) for t in ends[py]]
                to = slice(y * TOK_W, (y + 1) * TOK_W)
                first = sub80 == 0
                low[0] = jnp.where(first, 0.0, low[0])
                low[2] = jnp.where(first & (lane80 < 64), 0.0, low[2])
                end[1] = jnp.zeros_like(end[1])
                end[2] = jnp.where(lanes(8) < 64, end[2], 0.0)
                for k in range(3):
                    m = mid[k].astype(BF)
                    xe[f, to, k * 128 : k * 128 + 128] = low[k].astype(BF)
                    xe[f, to, 384 + k * 128 : 512 + k * 128] = m
                    xo[f, to, k * 128 : k * 128 + 128] = m
                    last = end[k][f * 3 + pair : f * 3 + pair + 1]
                    ahead = jnp.where(
                        sub80 == TOK_W - 1, last, pltpu.roll(low[k], TOK_W - 1, 0)
                    )
                    xo[f, to, 384 + k * 128 : 512 + k * 128] = ahead.astype(BF)

    bias_out = coutv_ref[...]
    copies = []
    for f in range(2):
        for side, x in enumerate((xe, xo)):
            acc = None
            for b in range(3):
                rows = slice(b * TOK_W, (b + 4) * TOK_W)
                ks = slice(b * 768, b * 768 + 768)
                term = jnp.dot(x[f, rows], cout_ref[1, ks], preferred_element_type=F32)
                acc = term if acc is None else acc + term
                if f == 1:
                    acc = acc + jnp.dot(x[0, rows], cout_ref[0, ks], preferred_element_type=F32)
            for j in range(4):
                for o in range(2):
                    lines[f, j, pl.ds(2 * side + o, TOK_W, stride=4), :] = (
                        acc[j * TOK_W : (j + 1) * TOK_W, o * 128 : o * 128 + 128] + bias_out
                    )
        for j in range(4):
            outs[f, j] = lines[f, j].T[0:96].astype(BF)
        copy = pltpu.make_async_copy(outs.at[f], out_ref.at[f], sems.at[f])
        copy.start()
        copies.append(copy)
    for copy in copies:
        copy.wait()


def decode(group, flags, pieces, table, const, cin, cinv, up, upv, cout, coutv):
    vmem = pl.BlockSpec(memory_space=pltpu.VMEM)
    return pl.pallas_call(
        functools.partial(decode_kernel, float(group)),
        in_specs=[vmem] * 13,
        out_specs=pl.BlockSpec(memory_space=pltpu.HBM),
        out_shape=jax.ShapeDtypeStruct((2, 4, 96, 4 * TOK_W), BF),
        scratch_shapes=[
            pltpu.VMEM((6 * TOK_W, 1536), BF),
            pltpu.VMEM((6 * TOK_W + 16, 1536), BF),
            pltpu.VMEM((8, 1536), F32),
            pltpu.VMEM((6 * TOK_W, 768), F32),
            pltpu.VMEM((6 * TOK_W + 16, 768), F32),
            pltpu.VMEM((2, 6 * TOK_W, 768), BF),
            pltpu.VMEM((2, 6 * TOK_W, 768), BF),
            pltpu.VMEM((2, 4, 4 * TOK_W, 128), F32),
            pltpu.VMEM((2, 4, 96, 4 * TOK_W), BF),
            pltpu.SemaphoreType.DMA((2,)),
        ],
        compiler_params=pltpu.CompilerParams(vmem_limit_bytes=24 << 20),
        cost_estimate=pl.CostEstimate(
            flops=5_000_000_000, bytes_accessed=8_000_000, transcendentals=1_300_000
        ),
        name="decode",
    )(flags, *pieces, table, const, cin, cinv, up, upv, cout, coutv)


def exchange(block, mask, count):
    return lax.ppermute(block, "seq", [(i, i ^ mask) for i in range(count)])


def merged(own, received):
    total = own[:, :HALF].astype(F32)
    for item in received:
        total = total + item[:, :HALF].astype(F32)
    return jnp.concatenate(
        [total.astype(BF), own[:, HALF:]] + [item[:, HALF:] for item in received], axis=1
    )


def cut(block, start, size):
    return lax.dynamic_slice_in_dim(block, start, size, 0)


def last_kernel(count, placing, unit, *refs):
    block_ref, *received, out0, out1, out2, out3, held = refs
    size = received[0].shape[0]
    me = lax.axis_index("seq")

    def window(step, extent):
        return jnp.clip(me // step * step - 1, 0, count - extent)

    old_size, old_unit = placing
    new = window(unit, size)
    old = window(old_unit, old_size) if old_unit else 0
    nothing = jnp.zeros(held.shape[1:], BF)
    held[0] = nothing
    held[size + 1] = nothing
    for i in range(size):
        own = block_ref[new - old + i].astype(F32)
        others = [item[i].astype(F32) for item in received]
        total = own[:HALF]
        for item in others:
            total = total + item[:HALF]
        held[i + 1] = jnp.concatenate(
            [total, own[HALF:]] + [item[HALF:] for item in others], axis=0
        ).astype(BF)
    for mask, out in ((0, out0), (2, out1), (1, out2), (3, out3)):
        first = (me ^ mask) - new
        for j in range(3):
            out[j] = held[first + j]


def last_sums(block, received, count, placing, unit):
    rows = block.shape[1] + len(received) * (received[0].shape[1] - HALF)
    vmem = pl.BlockSpec(memory_space=pltpu.VMEM)
    return pl.pallas_call(
        functools.partial(last_kernel, count, placing, unit),
        in_specs=[vmem] * (1 + len(received)),
        out_specs=[vmem] * 4,
        out_shape=[jax.ShapeDtypeStruct((3, rows, 128), BF)] * 4,
        scratch_shapes=[pltpu.VMEM((received[0].shape[0] + 2, rows, 128), BF)],
        compiler_params=pltpu.CompilerParams(vmem_limit_bytes=16 << 20),
        name="last_sums",
    )(block, *received)


def steps_of(count):
    bit = count.bit_length() - 3
    steps = [[2 << bit, 1 << bit, 3 << bit]]
    while bit > 2:
        bit -= 1
        steps.append([1 << bit])
    return steps


def device_order(count):
    order = [0]
    for masks in steps_of(count):
        order = order + [o ^ mask for mask in masks for o in order]
    order = order + [o ^ 2 for o in order]
    return np.asarray([o + c for o in order for c in range(2)], np.int32)


def gather_rows(own, give, weights, ready, me, count):
    block = (own.astype(F32) + exchange(give, 1, count).astype(F32)).astype(BF)
    block, weights = lax.optimization_barrier((block, weights))

    def window(base, size):
        return jnp.clip(base - 1, 0, count - size)

    start = jnp.int32(0)
    steps = steps_of(count)
    placing = (count, 0)
    for number, masks in enumerate(steps):
        unit = min(masks)
        size = unit + 2
        base = (me // unit) * unit
        new = window(base, size)
        received = [
            exchange(cut(block, window(base ^ mask, size) - start, size), mask, count)
            for mask in masks
        ]
        if number == len(steps) - 1:
            block = last_sums(block, received, count, placing, unit)
        else:
            block = merged(cut(block, new - start, size), received)
        if number == 0:
            block, weights = lax.optimization_barrier((block, ready(weights)))
        start = new
        placing = (size, unit)
    pieces = [block[0]] + [
        exchange(piece, mask, count) for piece, mask in zip(block[1:], (2, 1, 3), strict=True)
    ]
    return pieces, weights


def local(
    hidden,
    mod_shift,
    mod_scale,
    head_weight,
    head_bias,
    conv_in_weight,
    conv_in_bias,
    gain_in,
    up_weight,
    up_bias,
    gain_up,
    out_weight,
    out_bias,
):
    count = lax.axis_size("seq")
    me = lax.axis_index("seq")
    feats = hidden.shape[1]
    flags = jnp.stack([me % 2 == 0, me > 0, me < count - 1]).astype(F32)
    flags = jnp.broadcast_to(flags[:, None], (3, 384))
    own, give = project(hidden, head_weight, mod_scale[None])
    weights = (head_weight, conv_in_weight, jnp.swapaxes(up_weight, 2, 3), out_weight)

    def ready(parts):
        head_again, cin, up, cout = parts
        return flags, prepare(
            head_again, mod_scale[None], mod_shift[None], head_bias[None],
            (((me // 2) * 2) ^ device_order(count))[:, None],
            cin, up, jnp.stack([up_bias, gain_up]), cout,
        )

    pieces, weights = gather_rows(own, give, weights, ready, me, count)
    flags, (table, const, cin, up, upv, cout) = weights
    cinv = jnp.stack([conv_in_bias, gain_in])
    coutv = jnp.pad(out_bias, (0, 32))[None]
    out = decode(feats, flags, pieces, table, const, cin, cinv, up, upv, cout, coutv)
    return jnp.swapaxes(out, 2, 3)


def solution(mesh):
    placed = (P("grp", "seq", None), P(), P(), P(), P(), P(), P(), P(), P(), P(), P(), P(), P())
    return jax.shard_map(
        local, mesh=mesh, in_specs=placed, out_specs=P("grp", "seq", None, None), check_vma=False
    )
```
